128 devices in a mesh: ctx: 64 (over y, x, z), head: 2 (over core).
Axes of the slice: x: 4, y: 4, z: 4, core: 2. Of those that a mesh axis runs over, the one named last changes fastest.
Arguments:
- queries: bfloat16 [32768, 4096], P('ctx', 'head'), may hold values from -24 to 24
- keys: bfloat16 [32768, 1024], P('ctx', 'head'), may hold values from -24 to 24
- values: bfloat16 [32768, 1024], P('ctx', 'head'), may hold values from -40 to 40
- token_log_decay: float32 [8, 32768], P('head', 'ctx'), may hold values from -1 to 0
- seq_ids: int32 [32768], P('ctx'), may hold values from 0 to 7, never falling along the last dimension, each value on 1 to 24576 neighbouring positions
- norm_gain: float32 [4096], P('head'), may hold values from 0.1 to 0.4
Outputs:
- combined: bfloat16 [32768, 4096], P('ctx', 'head')
The draws below stay inside these ranges and needn't reach their ends.
Inputs may be any that keep to these rules, and one draw needn't show every extreme that they name: `seq_ids`: each sequence is one contiguous run of tokens and the numbers never fall; no run is longer than 24576 tokens and one has exactly 24576.
All inputs are finite; a program needn't handle non-finite values.
Results may differ from the reference program's by a relative error of at most 0.0075.
Values may be sent and summed in bfloat16 or wider, within the bound.
A program may use at most 192 MiB of HBM per device.

```python
import math
import jax
import jax.numpy as jnp
import numpy as np
from jax import lax

QUERY_HEADS = 32
KEY_VALUE_HEADS = 8
HEAD_SIZE = 128
WINDOW_LENGTH = 2048
TOKENS_PER_CTX = 512
TOKEN_TOTAL = 32768
NSEQ = 8
LONGEST_LENGTH = 24576


def draw_keys(key, part):
    normal_sample = jnp.clip(jax.random.normal(jax.random.fold_in(key, 2), (TOKEN_TOTAL, KEY_VALUE_HEADS * HEAD_SIZE), jnp.float32), -6.0, 6.0)
    return normal_sample.astype(jnp.bfloat16)


def draw_queries(key, part):
    normal_sample = 2.0 * jnp.clip(jax.random.normal(jax.random.fold_in(key, 1), (TOKEN_TOTAL, QUERY_HEADS * HEAD_SIZE), jnp.float32), -6.0, 6.0)
    return normal_sample.astype(jnp.bfloat16)


def draw_values(key, part):
    random_key_normal, random_key_jitter = jax.random.split(jax.random.fold_in(key, 3))
    normal_sample = jnp.clip(jax.random.normal(random_key_normal, (TOKEN_TOTAL, KEY_VALUE_HEADS * HEAD_SIZE), jnp.float32), -6.0, 6.0)
    head_linear_ramp = (jnp.arange(KEY_VALUE_HEADS * HEAD_SIZE) // HEAD_SIZE).astype(jnp.float32) / max(KEY_VALUE_HEADS - 1, 1) - 0.5
    column_jitter = jnp.exp(jax.random.uniform(random_key_jitter, (KEY_VALUE_HEADS * HEAD_SIZE,), jnp.float32, math.log(0.5), math.log(2.0)))
    column_scale = jnp.power(3.0, head_linear_ramp) * column_jitter
    return (normal_sample * column_scale[None, :]).astype(jnp.bfloat16)


def draw_token_log_decay(key, part):
    random_key_quick, random_key_speed, random_key_gentle, random_key_jagged, random_key_block, random_key_spike, random_key_decay = jax.random.split(jax.random.fold_in(key, 4), 7)
    quick_head_fraction = 0.5
    quick_decay_heads = jax.random.uniform(random_key_quick, (KEY_VALUE_HEADS, 1), jnp.float32) < quick_head_fraction
    quick_decay_rate = jax.random.uniform(random_key_speed, (KEY_VALUE_HEADS, 1), jnp.float32, 1.0 / 50.0, 1.0 / 30.0)
    gentle_decay_rate = jax.random.uniform(random_key_gentle, (KEY_VALUE_HEADS, 1), jnp.float32, 0.1, 0.5) * math.log(10.0) / LONGEST_LENGTH
    head_decay_rate = jnp.where(quick_decay_heads, quick_decay_rate, gentle_decay_rate)
    jaggedness = jax.random.uniform(random_key_jagged, (KEY_VALUE_HEADS, TOKEN_TOTAL), jnp.float32, 0.5, 1.5)
    block_decay_factor = jnp.exp(jax.random.uniform(random_key_block, (KEY_VALUE_HEADS, TOKEN_TOTAL // TOKENS_PER_CTX), jnp.float32, math.log(0.5), math.log(2.0)))
    block_decay_factor = jnp.repeat(block_decay_factor, TOKENS_PER_CTX, axis=1)
    spike_token_mask = jax.random.uniform(random_key_spike, (1, TOKEN_TOTAL), jnp.float32) < 4.0 / TOKEN_TOTAL
    spike_decay_loss = jnp.log(jax.random.uniform(random_key_decay, (1, TOKEN_TOTAL), jnp.float32, 0.5, 0.8))
    return -head_decay_rate * jaggedness * block_decay_factor + jnp.where(spike_token_mask, spike_decay_loss, 0.0)


def block_scale(rng, dims, shards, low, largest):
    gain, own = 1.0, jax.random.fold_in(rng, 6)
    for position, blocks in shards:
        draws = jnp.exp(jax.random.uniform(jax.random.fold_in(own, position), (blocks,), jnp.float32, low / len(shards), largest / len(shards)))
        gain = gain * jnp.repeat(draws, dims[position] // blocks).reshape([-1 if axis == position else 1 for axis in range(len(dims))])
    return gain


def length_profile(number_of, total, limit, lean):
    loads = [(1 << 20) // math.isqrt(standing ** lean) + 1 for standing in range(2, number_of + 1)]
    rest, given = total - limit - (number_of - 1), [1] * (number_of - 1)
    while rest > 0:
        movable = [i for i in range(number_of - 1) if given[i] < limit]
        pool, left = sum([loads[i] for i in movable]), rest
        for i in movable:
            more = min(limit - given[i], max(1, left * loads[i] // pool), rest)
            given[i] = given[i] + more
            rest = rest - more
    return np.array([limit] + given)


def ragged_sizes(key, number_of, total, limit, skew):
    if number_of == 2:
        one = jax.random.randint(key, (), max(1, total - limit), min(limit, total - 1) + 1)
        return jnp.stack([one, total - one])
    sizes = jnp.asarray(length_profile(number_of, total, limit, skew), jnp.int32)
    twos = (number_of - 1) // 2
    source_of, receiver = sizes[1:1 + 2 * twos:2], sizes[2:2 + 2 * twos:2]
    margin = jnp.minimum(source_of - 1, limit - receiver)
    passed = jax.random.randint(jax.random.fold_in(key, 1), (twos,), 0, 1 << 20) % (margin + 1)
    sizes = sizes.at[1:1 + 2 * twos:2].set(source_of - passed).at[2:2 + 2 * twos:2].set(receiver + passed)
    return sizes[jax.random.permutation(jax.random.fold_in(key, 2), number_of)]


def setup_inputs(seed: int = 0) -> dict:
    arg_keys = jax.random.split(jax.random.key(seed), 7)
    queries = draw_queries(jax.random.fold_in(arg_keys[6], 71), 0)
    keys = draw_keys(jax.random.fold_in(arg_keys[6], 71), 0)
    values = draw_values(jax.random.fold_in(arg_keys[6], 71), 0)
    token_log_decay = draw_token_log_decay(jax.random.fold_in(arg_keys[6], 71), 0)
    seq_ids = jnp.searchsorted(jnp.cumsum(ragged_sizes(arg_keys[4], NSEQ, TOKEN_TOTAL, LONGEST_LENGTH, 2)), jnp.arange(TOKEN_TOTAL), side="right").astype(jnp.int32)
    norm_gain = jnp.clip(0.1 + 0.3 * jax.random.uniform(arg_keys[5], (QUERY_HEADS * HEAD_SIZE,), jnp.float32) ** block_scale(arg_keys[5], (QUERY_HEADS * HEAD_SIZE,), ((0, 2),), -0.2, 0.2), 0.1, 0.4)
    return dict(queries=queries, keys=keys, values=values, token_log_decay=token_log_decay, seq_ids=seq_ids, norm_gain=norm_gain)


def linear_part(queries, keys, values, token_log_decay, seq_ids):
    number_of_blocks = TOKEN_TOTAL // TOKENS_PER_CTX
    query_groups = QUERY_HEADS // KEY_VALUE_HEADS
    query_block_list = queries.reshape(number_of_blocks, TOKENS_PER_CTX, KEY_VALUE_HEADS, query_groups, HEAD_SIZE)
    key_block_list = keys.reshape(number_of_blocks, TOKENS_PER_CTX, KEY_VALUE_HEADS, HEAD_SIZE)
    value_block_list = values.reshape(number_of_blocks, TOKENS_PER_CTX, KEY_VALUE_HEADS, HEAD_SIZE)
    decay_blocks = token_log_decay.reshape(KEY_VALUE_HEADS, number_of_blocks, TOKENS_PER_CTX).transpose(1, 0, 2)
    id_blocks = seq_ids.reshape(number_of_blocks, TOKENS_PER_CTX)
    positions = jnp.arange(TOKENS_PER_CTX, dtype=jnp.int32)
    lower_mask = positions[:, None] >= positions[None, :]

    def advance(carried, block_data):
        kv_state, prev_id = carried
        single_query_block, single_key_block, single_value_block, g_block, id_block = block_data
        q_float = single_query_block.astype(jnp.float32)
        k_float = single_key_block.astype(jnp.float32)
        v_float = single_value_block.astype(jnp.float32)
        cumulative = jnp.cumsum(g_block, axis=1)
        linked = lower_mask & (id_block[:, None] == id_block[None, :])
        exponent = jnp.where(linked[None], cumulative[:, :, None] - cumulative[:, None, :], 0.0)
        decays = jnp.where(linked[None], jnp.exp(exponent), 0.0)
        qk_dots = jnp.einsum('thgd,shd->hgts', q_float, k_float, precision=lax.Precision.HIGHEST)
        inner_term = jnp.einsum('hgts,shd->thgd', qk_dots * decays[:, None], v_float, precision=lax.Precision.HIGHEST)
        entry_factor = jnp.exp(cumulative) * (id_block == prev_id)[None, :].astype(jnp.float32)
        cross_term = jnp.einsum('thgd,hde->thge', q_float, kv_state, precision=lax.Precision.HIGHEST) * entry_factor.T[:, :, None, None]
        last_id = id_block[TOKENS_PER_CTX - 1]
        tail_weight = jnp.where(id_block[None, :] == last_id, jnp.exp(cumulative[:, -1:] - cumulative), 0.0)
        local_state = jnp.einsum('shd,she->hde', k_float * tail_weight.T[:, :, None], v_float, precision=lax.Precision.HIGHEST)
        carry_factor = jnp.exp(cumulative[:, -1]) * (last_id == prev_id).astype(jnp.float32)
        new_state = carry_factor[:, None, None] * kv_state + local_state
        linear_out = (inner_term + cross_term).reshape(TOKENS_PER_CTX, QUERY_HEADS * HEAD_SIZE)
        return ((new_state, last_id), linear_out)
    initial_state = (jnp.zeros((KEY_VALUE_HEADS, HEAD_SIZE, HEAD_SIZE), jnp.float32), jnp.array(-1, dtype=jnp.int32))
    _, outputs = lax.scan(advance, initial_state, (query_block_list, key_block_list, value_block_list, decay_blocks, id_blocks))
    return outputs.reshape(TOKEN_TOTAL, QUERY_HEADS * HEAD_SIZE)

def window_part(queries, keys, values, seq_ids):
    query_groups = QUERY_HEADS // KEY_VALUE_HEADS
    random_key_extent = WINDOW_LENGTH + TOKENS_PER_CTX
    score_scale = 1.0 / math.sqrt(HEAD_SIZE)
    padded_keys = jnp.concatenate([jnp.zeros((WINDOW_LENGTH, KEY_VALUE_HEADS * HEAD_SIZE), keys.dtype), keys], 0)
    padded_values = jnp.concatenate([jnp.zeros((WINDOW_LENGTH, KEY_VALUE_HEADS * HEAD_SIZE), values.dtype), values], 0)
    pad_ids = jnp.concatenate([jnp.full((WINDOW_LENGTH,), -1, dtype=jnp.int32), seq_ids], 0)

    def one_block(block_index):
        first_row_position = (block_index * TOKENS_PER_CTX).astype(jnp.int32)
        single_query_block = lax.dynamic_slice_in_dim(queries, first_row_position, TOKENS_PER_CTX, 0).reshape(TOKENS_PER_CTX, KEY_VALUE_HEADS, query_groups, HEAD_SIZE).astype(jnp.float32)
        single_key_block = lax.dynamic_slice_in_dim(padded_keys, first_row_position, random_key_extent, 0).reshape(random_key_extent, KEY_VALUE_HEADS, HEAD_SIZE).astype(jnp.float32)
        single_value_block = lax.dynamic_slice_in_dim(padded_values, first_row_position, random_key_extent, 0).reshape(random_key_extent, KEY_VALUE_HEADS, HEAD_SIZE).astype(jnp.float32)
        key_ids = lax.dynamic_slice_in_dim(pad_ids, first_row_position, random_key_extent, 0)
        query_ids = lax.dynamic_slice_in_dim(seq_ids, first_row_position, TOKENS_PER_CTX, 0)
        q_pos = first_row_position + jnp.arange(TOKENS_PER_CTX, dtype=jnp.int32)
        k_pos = first_row_position - WINDOW_LENGTH + jnp.arange(random_key_extent, dtype=jnp.int32)
        distance = q_pos[:, None] - k_pos[None, :]
        allowed = (k_pos[None, :] >= 0) & (distance >= 0) & (distance < WINDOW_LENGTH) & (query_ids[:, None] == key_ids[None, :])
        allowed = allowed[:, None, None, :]
        scores = jnp.einsum('thgd,khd->thgk', single_query_block, single_key_block, precision=lax.Precision.HIGHEST) * score_scale
        scores = jnp.where(allowed, scores, -1e+30)
        row_max = lax.optimization_barrier(jnp.max(scores, axis=3, keepdims=True))
        exp_scores = jnp.where(allowed, jnp.exp(scores - row_max), 0.0)
        weights = (exp_scores / lax.optimization_barrier(jnp.sum(exp_scores, axis=3, keepdims=True))).astype(jnp.bfloat16)
        head_out = jnp.einsum('thgk,khd->thgd', weights.astype(jnp.float32), single_value_block, precision=lax.Precision.HIGHEST)
        return head_out.reshape(TOKENS_PER_CTX, QUERY_HEADS * HEAD_SIZE)
    outputs = lax.map(one_block, jnp.arange(TOKEN_TOTAL // TOKENS_PER_CTX, dtype=jnp.int32))
    return outputs.reshape(TOKEN_TOTAL, QUERY_HEADS * HEAD_SIZE)

def reference(queries, keys, values, token_log_decay, seq_ids, norm_gain):
    linear_out = linear_part(queries, keys, values, token_log_decay, seq_ids)
    window_out = window_part(queries, keys, values, seq_ids)
    mean_square = lax.optimization_barrier(jnp.mean(linear_out * linear_out, axis=1))
    normed = linear_out * lax.rsqrt(mean_square + 1e-06)[:, None]
    return (window_out + norm_gain[None, :] * normed).astype(jnp.bfloat16)
```

```python
import math

import jax
import jax.numpy as jnp
from jax import lax
from jax.experimental import pallas as pl
from jax.experimental.pallas import tpu as pltpu
from jax.sharding import PartitionSpec as P

QUERY_HEADS = 32
KEY_VALUE_HEADS = 8
HEAD_SIZE = 128
WINDOW_LENGTH = 2048
LOG2E = 1.4426950408889634
SCALE = LOG2E / math.sqrt(HEAD_SIZE)
HIDDEN = -1e30
SMALL, LARGE = 2.0**-60, 2.0**110
MESH = pl.DeviceIdType.MESH
F32, BF16 = jnp.float32, jnp.bfloat16
T = 512
H = HEAD_SIZE
KV = 4
G = 4
STATE_ROWS = H + 16


def nt(a, b):
    return lax.dot_general(a, b, (((1,), (1,)), ((), ())), preferred_element_type=F32)


def nn(a, b):
    return lax.dot_general(a, b, (((1,), (0,)), ((), ())), preferred_element_type=F32)


def tn(a, b):
    return lax.dot_general(a, b, (((0,), (0,)), ((), ())), preferred_element_type=F32)


def pack_state(state, factor):
    high = factor.astype(BF16).astype(F32)
    middle = (factor - high).astype(BF16).astype(F32)
    low = factor - high - middle
    row = lax.broadcasted_iota(jnp.int32, (16, H), 0)
    tail = jnp.where(row < 4, high, jnp.where(row < 8, middle, low))
    return jnp.concatenate([state, tail], 0).astype(BF16)


def unpack_state(message):
    tail = message[H:, :].astype(F32)
    return message[:H, :].astype(F32), tail[0:1] + tail[4:5] + tail[8:9]


def head_columns(index):
    return pl.ds(pl.multiple_of(index * H, H), H)


def main_kernel(
    q_hbm, k_hbm, v_hbm, decay, ids, gain,
    out_hbm, flag, k_all, v_all, states_in, inverse_out, columns_out, rows_out,
    q, kb, vb, rk, rv, rid, acc, total, lin, causal, later, cum, alive_ref, squares, partner,
    sa, ra, rx, ry, sd, rd, sx, sy, outb, own_decay,
    in_sem, q_sem, out_sem, save_sem, ids_s, ids_r, block_s, block_r,
    st_s, st_r, sq_s, sq_r,
):
    me = lax.axis_index("ctx")
    core = lax.axis_index("head")
    z = lax.rem(me, 4)
    x = lax.rem(me // 4, 4)
    y = me // 16
    line = me - z

    def dev(ctx):
        return {"ctx": ctx, "head": core}

    def around(offset):
        return lax.rem(me + (offset + 64), 64)

    def on_line(position):
        return line + position

    def on_x(position):
        return y * 16 + position * 4 + z

    def on_y(position):
        return position * 16 + x * 4 + z

    def own_chunk(head, kind):
        source, target = ((k_hbm, kb), (v_hbm, vb))[kind]
        return pltpu.make_async_copy(
            source.at[:, pl.ds(head * H, H)], target.at[head], in_sem.at[head, kind]
        )

    chunk_order = (2, 0, 3, 1)
    for head in chunk_order:
        own_chunk(head, 0).start()
        own_chunk(head, 1).start()
    q_copy = pltpu.make_async_copy(q_hbm, q, q_sem)
    q_copy.start()

    barrier = pltpu.get_barrier_semaphore()
    for offset in (1, 2, 3, 4, -1, -2, -3, -4):
        pl.semaphore_signal(barrier, inc=1, device_id=dev(around(offset)), device_id_type=MESH)
    for step in (1, 2, 3):
        for ctx in (
            on_line(lax.rem(z + step, 4)),
            on_x(lax.rem(x + step, 4)),
            on_y(lax.rem(y + step, 4)),
        ):
            pl.semaphore_signal(barrier, inc=1, device_id=dev(ctx), device_id_type=MESH)
    other = {"ctx": me, "head": 1 - core}
    pl.semaphore_signal(barrier, inc=1, device_id=other, device_id_type=MESH)
    pl.semaphore_wait(barrier, 18)

    def id_copy(back):
        return pltpu.make_async_remote_copy(
            src_ref=ids, dst_ref=rid.at[back - 1], send_sem=ids_s.at[back - 1],
            recv_sem=ids_r.at[back - 1], device_id=dev(around(back)), device_id_type=MESH,
        )

    for back in (1, 2, 3, 4):
        id_copy(back).start()

    to_four = around(4)
    to_one = jnp.where(z < 3, around(1), on_line(0))
    to_three = jnp.where(z > 0, around(-1), on_line(3))

    def block_copy(source, back, head, kind, target):
        return pltpu.make_async_remote_copy(
            src_ref=source, dst_ref=(rk, rv)[kind].at[back - 1, head],
            send_sem=block_s.at[back - 1, head, kind], recv_sem=block_r.at[back - 1, head, kind],
            device_id=dev(target), device_id_type=MESH,
        )

    def own_send(step, kind):
        early, late = (step + 2) % 4, step
        block_copy((kb, vb)[kind].at[early], 4, early, kind, to_four).start()

        @pl.when(z < 3)
        def _():
            block_copy((kb, vb)[kind].at[late], 1, late, kind, to_one).start()

        @pl.when(z == 0)
        def _():
            block_copy((kb, vb)[kind].at[early], 3, early, kind, to_three).start()

    def receive(back, head):
        for kind in (0, 1):
            block_copy((kb, vb)[kind].at[head], back, head, kind, to_four).wait_recv()

    def save(back, head):
        for kind in (0, 1):
            pltpu.make_async_copy(
                (rk, rv)[kind].at[back - 1, head], (k_all, v_all)[kind].at[back - 1, head],
                save_sem.at[back - 1, head, kind],
            ).start()

    def relay_four(head):
        receive(4, head)
        for kind in (0, 1):
            held = (rk, rv)[kind].at[3, head]

            @pl.when(z > 0)
            def _():
                block_copy(held, 3, head, kind, to_three).start()

            @pl.when(z == 3)
            def _():
                block_copy(held, 1, head, kind, to_one).start()

        save(4, head)

    def relay_two(head, source_back, target):
        for kind in (0, 1):
            held = (rk, rv)[kind].at[source_back - 1, head]
            block_copy(held, 2, head, kind, target).start()

    for head in chunk_order:
        own_chunk(head, 0).wait()
        own_chunk(head, 1).wait()
        if head == 0:
            own_send(0, 0)
            own_send(0, 1)

    running = decay[...]
    shift = 1
    lane = lax.broadcasted_iota(jnp.int32, (KV, T), 1)
    while shift < T:
        running = running + jnp.where(lane >= shift, pltpu.roll(running, shift, 1), 0.0)
        shift *= 2
    id_row = ids[...].astype(F32)
    rows = jnp.concatenate([running, id_row, jnp.zeros((3, T), F32)], 0)
    rows_out[...] = rows
    columns = jnp.concatenate([rows, jnp.zeros((H - 8, T), F32)], 0).T
    id_column = jnp.broadcast_to(columns[:, 4:5], (T, H))
    for head in range(KV):
        cum[head] = jnp.broadcast_to(columns[:, head : head + 1], (T, H))
    for part in range(4):
        row_at = lax.broadcasted_iota(jnp.int32, (T, H), 0)
        column_at = lax.broadcasted_iota(jnp.int32, (T, H), 1) + part * H
        span = slice(part * H, (part + 1) * H)
        linked = (column_at <= row_at) & (id_column == id_row[:, span])
        causal[:, span] = jnp.where(linked, 0.0, HIDDEN)
        later[:, span] = jnp.where(column_at > row_at, 0.0, HIDDEN)
    last_id = id_row[:, T - 1 : T]
    own_tail = id_column == last_id

    for back in (1, 2, 3, 4):
        id_copy(back).wait_recv()
    prev_id = jnp.where(me > 0, rid[0].astype(F32)[:, T - 1 : T], -1.0)
    before = jnp.zeros((1, 1), F32)
    for back in (1, 2, 3, 4):
        same = (rid[back - 1].astype(F32) == prev_id).astype(F32)
        count = jnp.sum(same, axis=1, keepdims=True)
        before = before + jnp.where(me >= back, count, 0.0)
    alive = (id_column == prev_id).astype(F32)
    alive_ref[...] = alive
    lane_at = lax.broadcasted_iota(jnp.int32, (T, H), 1)
    columns_out[...] = jnp.where(
        lane_at == 5, alive, jnp.where(lane_at == 6, jnp.broadcast_to(before, (T, H)), columns)
    )
    own_carry = (last_id == prev_id).astype(F32)

    for head in range(KV):
        end = running[head : head + 1, T - 1 : T]
        weight = jnp.where(own_tail, jnp.exp(end - cum[head]), 0.0)
        weighted = (kb[head].astype(F32) * weight).astype(BF16)
        state = tn(weighted, vb[head])
        factor = jnp.broadcast_to(jnp.exp(end) * own_carry, (1, H))
        sa[head] = pack_state(state, factor)

    def state_copy(stage, source, target, slot, ctx):
        return pltpu.make_async_remote_copy(
            src_ref=source, dst_ref=target.at[slot], send_sem=st_s.at[stage, slot],
            recv_sem=st_r.at[stage, slot], device_id=dev(ctx), device_id_type=MESH,
        )

    def state_send(stage, step):
        if stage == 0:
            to = lax.rem(z + step, 4)
            return pltpu.make_async_remote_copy(
                src_ref=sa.at[to], dst_ref=ra.at[z], send_sem=st_s.at[0, step], recv_sem=st_r.at[0, step],
                device_id=dev(on_line(to)), device_id_type=MESH,
            )
        if stage == 1:
            return pltpu.make_async_remote_copy(
                src_ref=sx, dst_ref=rx.at[x], send_sem=st_s.at[1, step], recv_sem=st_r.at[1, step],
                device_id=dev(on_x(lax.rem(x + step, 4))), device_id_type=MESH,
            )
        if stage == 2:
            return pltpu.make_async_remote_copy(
                src_ref=sy, dst_ref=ry.at[y], send_sem=st_s.at[2, step], recv_sem=st_r.at[2, step],
                device_id=dev(on_y(lax.rem(y + step, 4))), device_id_type=MESH,
            )
        to = lax.rem(z + step, 4)
        return pltpu.make_async_remote_copy(
            src_ref=sd.at[to], dst_ref=rd.at[z], send_sem=st_s.at[3, step], recv_sem=st_r.at[3, step],
            device_id=dev(on_line(to)), device_id_type=MESH,
        )

    def start_stage(stage):
        for step in (1, 2, 3):
            state_send(stage, step).start()

    def finish_stage(stage):
        for step in (1, 2, 3):
            state_send(stage, step).wait_recv()

    ra[z] = sa[z]
    start_stage(0)

    def fold(messages, limit=None):
        state, factor = jnp.zeros((H, H), F32), jnp.ones((1, H), F32)
        for position in range(4):
            item, by = unpack_state(messages[position])
            fresh, grown = state * by + item, factor * by
            if limit is None:
                state, factor = fresh, grown
            else:
                state = jnp.where(position < limit, fresh, state)
        return state, factor

    def after_line():
        finish_stage(0)
        sx[...] = pack_state(*fold(ra))
        rx[x] = sx[...]
        start_stage(1)

    def after_x():
        finish_stage(1)
        sy[...] = pack_state(*fold(rx))
        ry[y] = sy[...]
        start_stage(2)

    def after_y():
        finish_stage(2)
        state, _ = fold(ry, y)
        for position in range(4):
            item, by = unpack_state(rx[position])
            state = jnp.where(position < x, state * by + item, state)
        for position in range(4):
            sd[position] = state.astype(BF16)
            item, by = unpack_state(ra[position])
            state = state * by + item
        rd[z] = sd[z]
        start_stage(3)

    q_copy.wait()

    def own_unit(head):
        keys, values = kb[head], vb[head]
        wide = jnp.concatenate([values, jnp.ones((T, H), BF16)], 1)
        row = rows_out[pl.ds(head, 1), :]
        for first in (0, 256):
            here, upto = slice(first, first + 256), first + 256
            column = cum[head, here, :]
            for part in range(0, upto, H):
                span = slice(part, part + H)
                own_decay[here, span] = jnp.exp(column - row[:, span] + causal[here, span])
        for first in (0, 256):
            here, upto = slice(first, first + 256), first + 256
            for member in range(G):
                at = head_columns(head * G + member)
                scores = nt(q[here, at], keys[:upto])
                grown = jnp.exp2(scores * SCALE + causal[here, :upto]).astype(BF16)
                mixed = nn(grown, wide[:upto])
                acc[here, at] = mixed[:, :H]
                total[here, at] = mixed[:, H:]
                lin[here, at] = nn((scores * own_decay[here, :upto]).astype(BF16), values[:upto])

    def masked_values(back, head):
        place = lax.broadcasted_iota(jnp.int32, (T, H), 0).astype(F32)
        kept = place >= back * float(T) - columns_out[0:1, 6:7]
        values = jnp.where(kept, rv[back - 1, head].astype(F32), 0.0)
        return jnp.concatenate([values, jnp.where(kept, 1.0, 0.0)], 1).astype(BF16)

    def gather(here, at, mixed):
        live = alive_ref[here, :] > 0.0
        acc[here, at] += jnp.where(live, mixed[:, :H], 0.0)
        total[here, at] += jnp.where(live, mixed[:, H:], 0.0)

    def far_unit(back, head):
        keys, wide = rk[back - 1, head], masked_values(back, head)
        for member in range(G):
            at = head_columns(head * G + member)
            grown = jnp.exp2(nt(q[:, at], keys) * SCALE).astype(BF16)
            gather(slice(0, T), at, nn(grown, wide))

    def oldest_unit(head):
        keys, wide = rk[3, head], masked_values(4, head)
        for first in (0, 256):
            here, since = slice(first, first + 256), slice(first, T)
            for member in range(G):
                at = head_columns(head * G + member)
                scores = nt(q[here, at], keys[since])
                grown = jnp.exp2(scores * SCALE + later[here, since]).astype(BF16)
                gather(here, at, nn(grown, wide[since]))

    own_send(1, 0)

    def own_step(head, carry):
        own_unit(head)

        @pl.when(head == 0)
        def _():
            own_send(1, 1)

        @pl.when(head == 1)
        def _():
            own_send(2, 0)
            after_line()
            relay_four(2)

        @pl.when(head == 2)
        def _():
            own_send(2, 1)

        @pl.when(head == 3)
        def _():
            own_send(3, 0)
            own_send(3, 1)
            relay_four(3)
            after_x()

        return carry

    lax.fori_loop(0, KV, own_step, 0)

    def near_step(step, carry):
        early = lax.rem(step + 2, 4)

        @pl.when(step >= 2)
        def _():
            relay_four(early)

        oldest_unit(early)
        receive(1, step)
        save(1, step)

        @pl.when(step < 2)
        def _():
            relay_two(step, 1, around(1))

        @pl.when(step >= 2)
        def _():
            receive(3, step)
            save(3, step)
            relay_two(step, 3, around(-1))

        @pl.when(step == 1)
        def _():
            after_y()

        far_unit(1, step)
        return carry

    lax.fori_loop(0, KV, near_step, 0)

    def cross():
        finish_stage(3)
        squares[...] = jnp.zeros((T, H), F32)

        def cross_step(head, carry):
            state = rd[head]
            states_in[head] = state.astype(F32)
            entry = jnp.exp(cum[head]) * alive_ref[...]
            part = squares[...]
            for member in range(G):
                at = head_columns(head * G + member)
                whole = lin[:, at] + nn(q[:, at], state) * entry
                lin[:, at] = whole
                part = part + whole * whole
            squares[...] = part
            return carry

        lax.fori_loop(0, KV, cross_step, 0)
        row_sum = jnp.sum(squares[...], axis=1, keepdims=True)
        squares[...] = jnp.broadcast_to(row_sum, (T, H))
        square_copy().start()

    def square_copy():
        return pltpu.make_async_remote_copy(
            src_ref=squares, dst_ref=partner, send_sem=sq_s, recv_sem=sq_r, device_id=other,
            device_id_type=MESH,
        )

    def out_copy(head):
        wide = pl.ds(pl.multiple_of(head * G * H, G * H), G * H)
        return pltpu.make_async_copy(outb.at[:, wide], out_hbm.at[:, wide], out_sem.at[head])

    def far_step(step, carry):
        back = jnp.where(step < 4, 3, 2)
        head = jnp.where(step < 4, lax.rem(step + 2, 4), lax.rem(step, 4))

        @pl.when((step == 2) | (step == 3))
        def _():
            receive(3, head)
            save(3, head)

        @pl.when(step == 4)
        def _():
            cross()

        @pl.when(step >= 4)
        def _():
            receive(2, head)
            save(2, head)

        @pl.when(step == 5)
        def _():
            square_copy().wait_recv()
            mean = (squares[...] + partner[...]) * (1.0 / (QUERY_HEADS * HEAD_SIZE))
            inverse_out[...] = lax.rsqrt(mean + 1e-06)
            flag[...] = jnp.zeros((8, H), F32)

        far_unit(back, head)

        return carry

    lax.fori_loop(0, 8, far_step, 0)

    def last_step(head, carry):
        for member in range(G):
            at = head_columns(head * G + member)
            mass = total[:, at]
            good = (mass >= SMALL) & (mass <= LARGE)
            flag[...] += jnp.sum(jnp.where(good, 0.0, 1.0).reshape(T // 8, 8, H), axis=0)
            mixed = acc[:, at] / mass + gain[:, at] * (lin[:, at] * inverse_out[...])
            outb[:, at] = mixed.astype(BF16)
        out_copy(head).start()
        return carry

    lax.fori_loop(0, KV, last_step, 0)

    for head in range(KV):
        out_copy(head).wait()
        for kind in (0, 1):
            for back in (1, 2, 3, 4):
                held = (rk, rv)[kind].at[back - 1, head]
                pltpu.make_async_copy(
                    held, (k_all, v_all)[kind].at[back - 1, head], save_sem.at[back - 1, head, kind]
                ).wait()
                block_copy(held, back, head, kind, to_four).wait_send()
    for back in (1, 2, 3, 4):
        id_copy(back).wait_send()
    for stage in range(4):
        for step in (1, 2, 3):
            state_send(stage, step).wait_send()
    square_copy().wait_send()


def finish_kernel(
    flag, cand, q_hbm, k_hbm, v_hbm, k_all, v_all, states_hbm, inverse_hbm, columns_hbm, rows_hbm, gain_hbm,
    out_hbm, q, ks, vs, outb, states_in, inverse, columns, rows, gain, sems,
):
    bad = jnp.max(flag[...]) > 0.0

    @pl.when(jnp.logical_not(bad))
    def _():
        pieces = [pl.ds(part * (T // 8), T // 8) for part in range(8)]
        arrive = [
            pltpu.make_async_copy(cand.at[piece], outb.at[piece], sems.at[part])
            for part, piece in enumerate(pieces)
        ]
        leave = [
            pltpu.make_async_copy(outb.at[piece], out_hbm.at[piece], sems.at[part])
            for part, piece in enumerate(pieces)
        ]
        for copy in arrive:
            copy.start()
        for there, onward in zip(arrive, leave):
            there.wait()
            onward.start()
        for copy in leave:
            copy.wait()

    @pl.when(bad)
    def _():
        def bring(source, target, sem):
            copy = pltpu.make_async_copy(source, target, sems.at[sem])
            copy.start()
            copy.wait()

        bring(q_hbm, q, 0)
        bring(states_hbm, states_in, 0)
        bring(inverse_hbm, inverse, 0)
        bring(columns_hbm, columns, 0)
        bring(rows_hbm, rows, 0)
        bring(gain_hbm, gain, 0)
        for head in range(KV):
            for source, whole, target in ((k_hbm, k_all, ks), (v_hbm, v_all, vs)):
                bring(source.at[:, pl.ds(head * H, H)], target.at[head, pl.ds(4 * T, T)], 0)
                for back in (1, 2, 3, 4):
                    bring(whole.at[back - 1, head], target.at[head, pl.ds((4 - back) * T, T)], 0)

        def query_step(index, carry):
            head = index // G
            at = head_columns(index)
            for first in range(0, T, 128):
                here = pl.ds(first, 128)
                queries = q[here, at]
                id_column, alive = columns[here, 4:5], columns[here, 5:6]
                before = columns[here, 6:7]
                spot = lax.broadcasted_iota(jnp.int32, (128, 5 * T), 1)
                turn = lax.broadcasted_iota(jnp.int32, (128, 5 * T), 0) + first
                inside = (spot > turn) & (spot <= turn + 4 * T)
                ids = jnp.concatenate([jnp.zeros((1, 4 * T), F32), rows[4:5, :]], 1)
                old = (alive > 0.0) & (spot.astype(F32) >= 4.0 * T - before)
                allowed = inside & (((spot < 4 * T) & old) | ((spot >= 4 * T) & (ids == id_column)))
                scores = nt(queries, ks[head]) * (1.0 / math.sqrt(HEAD_SIZE))
                scores = jnp.where(allowed, scores, HIDDEN)
                top = jnp.max(scores, axis=1, keepdims=True)
                grown = jnp.where(allowed, jnp.exp(scores - top), 0.0)
                weights = grown / jnp.sum(grown, axis=1, keepdims=True)
                window = nn(weights.astype(BF16), vs[head])
                row = rows[pl.ds(head, 1), :]
                lane = lax.broadcasted_iota(jnp.int32, (128, H), 1)
                column = jnp.sum(
                    jnp.where(lane == head, columns[here, :], 0.0), axis=1, keepdims=True
                )
                own_at = lax.broadcasted_iota(jnp.int32, (128, T), 1)
                own_turn = lax.broadcasted_iota(jnp.int32, (128, T), 0) + first
                linked = (own_at <= own_turn) & (rows[4:5, :] == id_column)
                gap = jnp.where(linked, column - row, 0.0)
                kept = jnp.where(linked, jnp.exp(gap), 0.0)
                dots = nt(queries, ks[head, pl.ds(4 * T, T)]) * kept
                linear = nn(dots.astype(BF16), vs[head, pl.ds(4 * T, T)])
                entry = jnp.exp(column) * alive
                linear = linear + nn(queries, states_in[head].astype(BF16)) * entry
                mixed = window + gain[:, at] * (linear * inverse[here, :])
                outb[here, at] = mixed.astype(BF16)
            return carry

        lax.fori_loop(0, KV * G, query_step, 0)
        bring(outb, out_hbm, 0)


def body(queries, keys, values, token_log_decay, seq_ids, norm_gain):
    any_spec = pl.BlockSpec(memory_space=pltpu.HBM)
    vmem_spec = pl.BlockSpec(memory_space=pltpu.VMEM)
    dma = pltpu.SemaphoreType.DMA
    gain = norm_gain.reshape(1, -1)
    ids = seq_ids.reshape(1, -1)
    wide = KV * G * H
    results = pl.pallas_call(
        main_kernel,
        out_shape=(
            jax.ShapeDtypeStruct((T, wide), BF16),
            jax.ShapeDtypeStruct((8, H), F32),
            jax.ShapeDtypeStruct((4, KV, T, H), BF16),
            jax.ShapeDtypeStruct((4, KV, T, H), BF16),
            jax.ShapeDtypeStruct((KV, H, H), F32),
            jax.ShapeDtypeStruct((T, H), F32),
            jax.ShapeDtypeStruct((T, H), F32),
            jax.ShapeDtypeStruct((8, T), F32),
        ),
        in_specs=[any_spec] * 3 + [vmem_spec] * 3,
        out_specs=(any_spec, vmem_spec, any_spec, any_spec, vmem_spec, vmem_spec, vmem_spec, vmem_spec),
        scratch_shapes=[
            pltpu.VMEM((T, wide), BF16),
            pltpu.VMEM((KV, T, H), BF16),
            pltpu.VMEM((KV, T, H), BF16),
            pltpu.VMEM((4, KV, T, H), BF16),
            pltpu.VMEM((4, KV, T, H), BF16),
            pltpu.VMEM((4, 1, T), jnp.int32),
            pltpu.VMEM((T, wide), F32),
            pltpu.VMEM((T, wide), F32),
            pltpu.VMEM((T, wide), F32),
            pltpu.VMEM((T, T), F32),
            pltpu.VMEM((T, T), F32),
            pltpu.VMEM((KV, T, H), F32),
            pltpu.VMEM((T, H), F32),
            pltpu.VMEM((T, H), F32),
            pltpu.VMEM((T, H), F32),
            pltpu.VMEM((4, STATE_ROWS, H), BF16),
            pltpu.VMEM((4, STATE_ROWS, H), BF16),
            pltpu.VMEM((4, STATE_ROWS, H), BF16),
            pltpu.VMEM((4, STATE_ROWS, H), BF16),
            pltpu.VMEM((4, H, H), BF16),
            pltpu.VMEM((4, H, H), BF16),
            pltpu.VMEM((STATE_ROWS, H), BF16),
            pltpu.VMEM((STATE_ROWS, H), BF16),
            pltpu.VMEM((T, wide), BF16),
            pltpu.VMEM((T, T), F32),
            dma((KV, 2)),
            dma,
            dma((KV,)),
            dma((4, KV, 2)),
            dma((4,)),
            dma((4,)),
            dma((4, KV, 2)),
            dma((4, KV, 2)),
            dma((4, 4)),
            dma((4, 4)),
            dma,
            dma,
        ],
        compiler_params=pltpu.CompilerParams(
            collective_id=0, has_side_effects=True, vmem_limit_bytes=56 << 20
        ),
        name="attend",
    )(queries, keys, values, token_log_decay, ids, gain)
    cand, flag, k_all, v_all, states_in, inverse, columns, rows = results
    return pl.pallas_call(
        finish_kernel,
        out_shape=jax.ShapeDtypeStruct((T, wide), BF16),
        in_specs=[vmem_spec] + [any_spec] * 11,
        out_specs=any_spec,
        scratch_shapes=[
            pltpu.VMEM((T, wide), BF16),
            pltpu.VMEM((KV, 5 * T, H), BF16),
            pltpu.VMEM((KV, 5 * T, H), BF16),
            pltpu.VMEM((T, wide), BF16),
            pltpu.VMEM((KV, H, H), F32),
            pltpu.VMEM((T, H), F32),
            pltpu.VMEM((T, H), F32),
            pltpu.VMEM((8, T), F32),
            pltpu.VMEM((1, wide), F32),
            dma((8,)),
        ],
        compiler_params=pltpu.CompilerParams(vmem_limit_bytes=56 << 20),
        name="finish",
    )(flag, cand, queries, keys, values, k_all, v_all, states_in, inverse, columns, rows, gain)


def solution(mesh):
    return jax.shard_map(
        body,
        mesh=mesh,
        in_specs=(
            P("ctx", "head"),
            P("ctx", "head"),
            P("ctx", "head"),
            P("head", "ctx"),
            P("ctx"),
            P("head"),
        ),
        out_specs=P("ctx", "head"),
        check_vma=False,
    )
```

```python
import math

import jax
import jax.numpy as jnp
from jax import lax
from jax.experimental import pallas as pl
from jax.experimental.pallas import tpu as pltpu
from jax.sharding import PartitionSpec as P

QUERY_HEADS = 32
KEY_VALUE_HEADS = 8
HEAD_SIZE = 128
WINDOW_LENGTH = 2048
LOG2E = 1.4426950408889634
SCALE = LOG2E / math.sqrt(HEAD_SIZE)
HIDDEN = -1e30
SMALL, LARGE = 2.0**-60, 2.0**110
MESH = pl.DeviceIdType.MESH
F32, BF16 = jnp.float32, jnp.bfloat16
T = 512
H = HEAD_SIZE
KV = 4
G = 4
STATE_ROWS = H + 16
ORDERS = (
    ((1, 0), (3, 2), (3, 3), (1, 1), (3, 0), (3, 1), (2, 0), (1, 2), (2, 1), (2, 2), (1, 3), (2, 3)),
    ((1, 0), (1, 1), (3, 2), (1, 2), (3, 3), (1, 3), (3, 0), (3, 1), (2, 0), (2, 1), (2, 2), (2, 3)),
    ((1, 0), (1, 1), (3, 0), (1, 2), (3, 1), (3, 2), (1, 3), (3, 3), (2, 0), (2, 1), (2, 2), (2, 3)),
    ((1, 0), (3, 2), (1, 1), (3, 3), (1, 2), (3, 0), (1, 3), (3, 1), (2, 0), (2, 1), (2, 2), (2, 3)),
)


def nt(a, b):
    return lax.dot_general(a, b, (((1,), (1,)), ((), ())), preferred_element_type=F32)


def nn(a, b):
    return lax.dot_general(a, b, (((1,), (0,)), ((), ())), preferred_element_type=F32)


def tn(a, b):
    return lax.dot_general(a, b, (((0,), (0,)), ((), ())), preferred_element_type=F32)


def pack_state(state, factor):
    high = factor.astype(BF16).astype(F32)
    middle = (factor - high).astype(BF16).astype(F32)
    low = factor - high - middle
    row = lax.broadcasted_iota(jnp.int32, (16, H), 0)
    tail = jnp.where(row < 4, high, jnp.where(row < 8, middle, low))
    return jnp.concatenate([state, tail], 0).astype(BF16)


def unpack_state(message):
    tail = message[H:, :].astype(F32)
    return message[:H, :].astype(F32), tail[0:1] + tail[4:5] + tail[8:9]


def head_columns(index):
    return pl.ds(pl.multiple_of(index * H, H), H)


def main_kernel(
    q_hbm, k_hbm, v_hbm, decay, ids, gain,
    out_hbm, flag, k_all, v_all, states_in, inverse_out, columns_out, rows_out,
    q, kb, vb, rk, rv, rid, acc, total, lin, causal, later, cum, alive_ref, squares, partner,
    sa, ra, rx, ry, sd, rd, sx, sy, outb, own_decay,
    sk, sv,
    in_sem, q_sem, out_sem, save_sem, ids_s, ids_r, block_s, block_r,
    st_s, st_r, sq_s, sq_r, stop_s, stop_r,
):
    me = lax.axis_index("ctx")
    core = lax.axis_index("head")
    z = lax.rem(me, 4)
    x = lax.rem(me // 4, 4)
    y = me // 16
    line = me - z

    def dev(ctx):
        return {"ctx": ctx, "head": core}

    def around(offset):
        return lax.rem(me + (offset + 64), 64)

    def on_line(position):
        return line + position

    def on_x(position):
        return y * 16 + position * 4 + z

    def on_y(position):
        return position * 16 + x * 4 + z

    def own_chunk(head, kind):
        source, target = ((k_hbm, kb), (v_hbm, vb))[kind]
        return pltpu.make_async_copy(
            source.at[:, pl.ds(head * H, H)], target.at[head], in_sem.at[head, kind]
        )

    chunk_order = (2, 0, 3, 1)
    for head in chunk_order:
        own_chunk(head, 0).start()
        own_chunk(head, 1).start()
    q_copy = pltpu.make_async_copy(q_hbm, q, q_sem)
    q_copy.start()

    barrier = pltpu.get_barrier_semaphore()
    for offset in (1, 2, 3, 4, -1, -2, -3, -4):
        pl.semaphore_signal(barrier, inc=1, device_id=dev(around(offset)), device_id_type=MESH)
    for step in (1, 2, 3):
        for ctx in (
            on_line(lax.rem(z + step, 4)),
            on_x(lax.rem(x + step, 4)),
            on_y(lax.rem(y + step, 4)),
        ):
            pl.semaphore_signal(barrier, inc=1, device_id=dev(ctx), device_id_type=MESH)
    other = {"ctx": me, "head": 1 - core}
    pl.semaphore_signal(barrier, inc=1, device_id=other, device_id_type=MESH)
    pl.semaphore_wait(barrier, 18)

    def id_copy(back):
        return pltpu.make_async_remote_copy(
            src_ref=ids, dst_ref=rid.at[back - 1], send_sem=ids_s.at[back - 1],
            recv_sem=ids_r.at[back - 1], device_id=dev(around(back)), device_id_type=MESH,
        )

    for back in (1, 2, 3, 4):
        id_copy(back).start()

    to_four = around(4)
    to_one = jnp.where(z < 3, around(1), on_line(0))
    to_three = jnp.where(z > 0, around(-1), on_line(3))

    def block_copy(source, back, head, kind, target):
        return pltpu.make_async_remote_copy(
            src_ref=source, dst_ref=(rk, rv)[kind].at[back - 1, head],
            send_sem=block_s.at[back - 1, head, kind], recv_sem=block_r.at[back - 1, head, kind],
            device_id=dev(target), device_id_type=MESH,
        )

    first_early = jnp.where(z < 3, 2, 0)

    def early_head(step):
        return lax.rem(first_early + step, 4)

    def own_send(step, kind):
        early, late = early_head(step), step
        block_copy((kb, vb)[kind].at[early], 4, early, kind, to_four).start()

        @pl.when(z < 3)
        def _():
            block_copy((kb, vb)[kind].at[late], 1, late, kind, to_one).start()

        @pl.when(z == 0)
        def _():
            block_copy((kb, vb)[kind].at[early], 3, early, kind, to_three).start()

    def receive(back, head):
        for kind in (0, 1):
            block_copy((kb, vb)[kind].at[head], back, head, kind, to_four).wait_recv()

    def save(back, head):
        for kind in (0, 1):
            pltpu.make_async_copy(
                (rk, rv)[kind].at[back - 1, head], (k_all, v_all)[kind].at[back - 1, head],
                save_sem.at[back - 1, head, kind],
            ).start()

    def relay_four(step):
        head = early_head(step)
        receive(4, head)
        for kind in (0, 1):
            held = (rk, rv)[kind].at[3, head]

            @pl.when(z == 3)
            def _():
                block_copy(held, 1, head, kind, to_one).start()

            @pl.when(z > 0)
            def _():
                block_copy(held, 3, head, kind, to_three).start()

        save(4, head)

    def stop_copy(source, head, kind, target):
        slot = lax.rem(head, 2)
        return pltpu.make_async_remote_copy(
            src_ref=source, dst_ref=(sk, sv)[kind].at[slot],
            send_sem=block_s.at[1, head, kind], recv_sem=stop_r.at[slot, kind],
            device_id=dev(target), device_id_type=MESH,
        )

    def relay_up(head):
        for kind in (0, 1):
            held = (rk, rv)[kind].at[0, head]

            @pl.when(z < 3)
            def _():
                block_copy(held, 2, head, kind, around(1)).start()

            @pl.when(z == 3)
            def _():
                stop_copy(held, head, kind, on_line(0)).start()

    def relay_down(head):
        for kind in (0, 1):
            held = (rk, rv)[kind].at[2, head]

            @pl.when(z > 0)
            def _():
                block_copy(held, 2, head, kind, around(-1)).start()

            @pl.when(z == 0)
            def _():
                stop_copy(held, head, kind, on_line(3)).start()

    onward_line = jnp.where(z == 0, around(4), around(-4))
    onward_first = jnp.where(z == 0, 0, 2)

    def onward_copy(slot, kind):
        head = onward_first + slot
        return pltpu.make_async_remote_copy(
            src_ref=(sk, sv)[kind].at[slot], dst_ref=(rk, rv)[kind].at[1, head],
            send_sem=stop_s.at[slot, kind], recv_sem=block_r.at[1, head, kind],
            device_id=dev(onward_line), device_id_type=MESH,
        )

    def hand_on(slot, at):
        @pl.when(z == at)
        def _():
            for kind in (0, 1):
                stop_copy((sk, sv)[kind].at[slot], slot, kind, on_line(0)).wait_recv()
                onward_copy(slot, kind).start()

    for head in chunk_order:
        own_chunk(head, 0).wait()
        own_chunk(head, 1).wait()
        if head == 0:
            own_send(0, 0)
            own_send(0, 1)
    own_send(1, 0)

    running = decay[...]
    shift = 1
    lane = lax.broadcasted_iota(jnp.int32, (KV, T), 1)
    while shift < T:
        running = running + jnp.where(lane >= shift, pltpu.roll(running, shift, 1), 0.0)
        shift *= 2
    id_row = ids[...].astype(F32)
    rows = jnp.concatenate([running, id_row, jnp.zeros((3, T), F32)], 0)
    rows_out[...] = rows
    columns = jnp.concatenate([rows, jnp.zeros((H - 8, T), F32)], 0).T
    id_column = jnp.broadcast_to(columns[:, 4:5], (T, H))
    for head in range(KV):
        cum[head] = jnp.broadcast_to(columns[:, head : head + 1], (T, H))
    for part in range(4):
        row_at = lax.broadcasted_iota(jnp.int32, (T, H), 0)
        column_at = lax.broadcasted_iota(jnp.int32, (T, H), 1) + part * H
        span = slice(part * H, (part + 1) * H)
        linked = (column_at <= row_at) & (id_column == id_row[:, span])
        causal[:, span] = jnp.where(linked, 0.0, HIDDEN)
        later[:, span] = jnp.where(column_at > row_at, 0.0, HIDDEN)
    last_id = id_row[:, T - 1 : T]
    own_tail = id_column == last_id

    for back in (1, 2, 3, 4):
        id_copy(back).wait_recv()
    prev_id = jnp.where(me > 0, rid[0].astype(F32)[:, T - 1 : T], -1.0)
    before = jnp.zeros((1, 1), F32)
    for back in (1, 2, 3, 4):
        same = (rid[back - 1].astype(F32) == prev_id).astype(F32)
        count = jnp.sum(same, axis=1, keepdims=True)
        before = before + jnp.where(me >= back, count, 0.0)
    alive = (id_column == prev_id).astype(F32)
    alive_ref[...] = alive
    lane_at = lax.broadcasted_iota(jnp.int32, (T, H), 1)
    columns_out[...] = jnp.where(
        lane_at == 5, alive, jnp.where(lane_at == 6, jnp.broadcast_to(before, (T, H)), columns)
    )
    own_carry = (last_id == prev_id).astype(F32)

    for head in range(KV):
        end = running[head : head + 1, T - 1 : T]
        weight = jnp.where(own_tail, jnp.exp(end - cum[head]), 0.0)
        weighted = (kb[head].astype(F32) * weight).astype(BF16)
        state = tn(weighted, vb[head])
        factor = jnp.broadcast_to(jnp.exp(end) * own_carry, (1, H))
        sa[head] = pack_state(state, factor)

    def state_copy(stage, source, target, slot, ctx):
        return pltpu.make_async_remote_copy(
            src_ref=source, dst_ref=target.at[slot], send_sem=st_s.at[stage, slot],
            recv_sem=st_r.at[stage, slot], device_id=dev(ctx), device_id_type=MESH,
        )

    def state_send(stage, step):
        if stage == 0:
            to = lax.rem(z + step, 4)
            return pltpu.make_async_remote_copy(
                src_ref=sa.at[to], dst_ref=ra.at[z], send_sem=st_s.at[0, step], recv_sem=st_r.at[0, step],
                device_id=dev(on_line(to)), device_id_type=MESH,
            )
        if stage == 1:
            return pltpu.make_async_remote_copy(
                src_ref=sx, dst_ref=rx.at[x], send_sem=st_s.at[1, step], recv_sem=st_r.at[1, step],
                device_id=dev(on_x(lax.rem(x + step, 4))), device_id_type=MESH,
            )
        if stage == 2:
            return pltpu.make_async_remote_copy(
                src_ref=sy, dst_ref=ry.at[y], send_sem=st_s.at[2, step], recv_sem=st_r.at[2, step],
                device_id=dev(on_y(lax.rem(y + step, 4))), device_id_type=MESH,
            )
        to = lax.rem(z + step, 4)
        return pltpu.make_async_remote_copy(
            src_ref=sd.at[to], dst_ref=rd.at[z], send_sem=st_s.at[3, step], recv_sem=st_r.at[3, step],
            device_id=dev(on_line(to)), device_id_type=MESH,
        )

    def start_stage(stage):
        for step in (1, 2, 3):
            state_send(stage, step).start()

    def finish_stage(stage):
        for step in (1, 2, 3):
            state_send(stage, step).wait_recv()

    ra[z] = sa[z]
    start_stage(0)

    def fold(messages, limit=None):
        state, factor = jnp.zeros((H, H), F32), jnp.ones((1, H), F32)
        for position in range(4):
            item, by = unpack_state(messages[position])
            fresh, grown = state * by + item, factor * by
            if limit is None:
                state, factor = fresh, grown
            else:
                state = jnp.where(position < limit, fresh, state)
        return state, factor

    def after_line():
        finish_stage(0)
        sx[...] = pack_state(*fold(ra))
        rx[x] = sx[...]
        start_stage(1)

    def after_x():
        finish_stage(1)
        sy[...] = pack_state(*fold(rx))
        ry[y] = sy[...]
        start_stage(2)

    def after_y():
        finish_stage(2)
        state, _ = fold(ry, y)
        for position in range(4):
            item, by = unpack_state(rx[position])
            state = jnp.where(position < x, state * by + item, state)
        for position in range(4):
            sd[position] = state.astype(BF16)
            item, by = unpack_state(ra[position])
            state = state * by + item
        rd[z] = sd[z]
        start_stage(3)

    q_copy.wait()

    def own_unit(head):
        keys, values = kb[head], vb[head]
        wide = jnp.concatenate([values, jnp.ones((T, H), BF16)], 1)
        row = rows_out[pl.ds(head, 1), :]
        for first in (0, 256):
            here, upto = slice(first, first + 256), first + 256
            column = cum[head, here, :]
            for part in range(0, upto, H):
                span = slice(part, part + H)
                own_decay[here, span] = jnp.exp(column - row[:, span] + causal[here, span])
        for first in (0, 256):
            here, upto = slice(first, first + 256), first + 256
            for member in range(G):
                at = head_columns(head * G + member)
                scores = nt(q[here, at], keys[:upto])
                grown = jnp.exp2(scores * SCALE + causal[here, :upto]).astype(BF16)
                mixed = nn(grown, wide[:upto])
                acc[here, at] = mixed[:, :H]
                total[here, at] = mixed[:, H:]
                lin[here, at] = nn((scores * own_decay[here, :upto]).astype(BF16), values[:upto])

    def masked_values(back, head):
        place = lax.broadcasted_iota(jnp.int32, (T, H), 0).astype(F32)
        kept = place >= back * float(T) - columns_out[0:1, 6:7]
        values = jnp.where(kept, rv[back - 1, head].astype(F32), 0.0)
        return jnp.concatenate([values, jnp.where(kept, 1.0, 0.0)], 1).astype(BF16)

    def gather(here, at, mixed):
        live = alive_ref[here, :] > 0.0
        acc[here, at] += jnp.where(live, mixed[:, :H], 0.0)
        total[here, at] += jnp.where(live, mixed[:, H:], 0.0)

    def far_unit(back, head):
        keys, wide = rk[back - 1, head], masked_values(back, head)
        for member in range(G):
            at = head_columns(head * G + member)
            grown = jnp.exp2(nt(q[:, at], keys) * SCALE).astype(BF16)
            gather(slice(0, T), at, nn(grown, wide))

    def oldest_unit(head):
        keys, wide = rk[3, head], masked_values(4, head)
        for first in (0, 256):
            here, since = slice(first, first + 256), slice(first, T)
            for member in range(G):
                at = head_columns(head * G + member)
                scores = nt(q[here, at], keys[since])
                grown = jnp.exp2(scores * SCALE + later[here, since]).astype(BF16)
                gather(here, at, nn(grown, wide[since]))

    relay_four(0)
    own_send(1, 1)

    def own_step(head, carry):
        own_unit(head)

        @pl.when(head == 0)
        def _():
            own_send(2, 0)

        @pl.when(head == 1)
        def _():
            after_line()
            own_send(2, 1)

        @pl.when(head == 2)
        def _():
            relay_four(1)
            own_send(3, 0)

        @pl.when(head == 3)
        def _():
            own_send(3, 1)
            receive(1, 0)
            relay_up(0)
            save(1, 0)

        return carry

    lax.fori_loop(0, KV, own_step, 0)

    def cross():
        finish_stage(3)
        squares[...] = jnp.zeros((T, H), F32)

        def cross_step(head, carry):
            state = rd[head]
            states_in[head] = state.astype(F32)
            entry = jnp.exp(cum[head]) * alive_ref[...]
            part = squares[...]
            for member in range(G):
                at = head_columns(head * G + member)
                whole = lin[:, at] + nn(q[:, at], state) * entry
                lin[:, at] = whole
                part = part + whole * whole
            squares[...] = part
            return carry

        lax.fori_loop(0, KV, cross_step, 0)
        row_sum = jnp.sum(squares[...], axis=1, keepdims=True)
        squares[...] = jnp.broadcast_to(row_sum, (T, H))
        square_copy().start()

    def square_copy():
        return pltpu.make_async_remote_copy(
            src_ref=squares, dst_ref=partner, send_sem=sq_s, recv_sem=sq_r, device_id=other,
            device_id_type=MESH,
        )

    def out_copy(head):
        wide = pl.ds(pl.multiple_of(head * G * H, G * H), G * H)
        return pltpu.make_async_copy(outb.at[:, wide], out_hbm.at[:, wide], out_sem.at[head])

    def listed(step):
        code = jnp.int32(0)
        for place, order in enumerate(ORDERS):
            mine = jnp.int32(0)
            for index, (back, head) in enumerate(order):
                mine = jnp.where(step == index, back * 4 + head, mine)
            code = jnp.where(z == place, mine, code)
        return code // 4, lax.rem(code, 4)

    def far_step(step, carry):
        back, head = listed(step)

        @pl.when(step == 0)
        def _():
            after_x()

        @pl.when(step == 1)
        def _():
            relay_four(2)

        @pl.when(step == 2)
        def _():
            after_y()
            hand_on(0, 0)

        @pl.when(step == 3)
        def _():
            relay_four(3)

        @pl.when(step == 6)
        def _():
            hand_on(1, 0)
            hand_on(0, 3)
            cross()

        @pl.when(step == 8)
        def _():
            hand_on(1, 3)
            square_copy().wait_recv()
            mean = (squares[...] + partner[...]) * (1.0 / (QUERY_HEADS * HEAD_SIZE))
            inverse_out[...] = lax.rsqrt(mean + 1e-06)
            flag[...] = jnp.zeros((8, H), F32)

        @pl.when((back != 1) | (head != 0))
        def _():
            receive(back, head)
            save(back, head)

        @pl.when((back == 1) & (head == 1))
        def _():
            relay_up(head)

        @pl.when((back == 3) & (head >= 2))
        def _():
            relay_down(head)

        far_unit(back, head)
        return carry

    def old_step(step, carry):
        oldest_unit(early_head(step))
        lax.fori_loop(2 * step, 2 * step + 2, far_step, 0)
        return carry

    def last_step(step, carry):
        far_step(step, carry)
        head = step - 8
        for member in range(G):
            at = head_columns(head * G + member)
            mass = total[:, at]
            good = (mass >= SMALL) & (mass <= LARGE)
            flag[...] += jnp.sum(jnp.where(good, 0.0, 1.0).reshape(T // 8, 8, H), axis=0)
            mixed = acc[:, at] / mass + gain[:, at] * (lin[:, at] * inverse_out[...])
            outb[:, at] = mixed.astype(BF16)
        out_copy(head).start()
        return carry

    lax.fori_loop(0, 4, old_step, 0)
    lax.fori_loop(8, 12, last_step, 0)

    for head in range(KV):
        out_copy(head).wait()
        for kind in (0, 1):
            for back in (1, 2, 3, 4):
                held = (rk, rv)[kind].at[back - 1, head]
                pltpu.make_async_copy(
                    held, (k_all, v_all)[kind].at[back - 1, head], save_sem.at[back - 1, head, kind]
                ).wait()
                block_copy(held, back, head, kind, to_four).wait_send()
    for back in (1, 2, 3, 4):
        id_copy(back).wait_send()
    for stage in range(4):
        for step in (1, 2, 3):
            state_send(stage, step).wait_send()
    square_copy().wait_send()

    @pl.when((z == 0) | (z == 3))
    def _():
        for slot in (0, 1):
            for kind in (0, 1):
                onward_copy(slot, kind).wait_send()


def finish_kernel(
    flag, cand, q_hbm, k_hbm, v_hbm, k_all, v_all, states_hbm, inverse_hbm, columns_hbm, rows_hbm, gain_hbm,
    out_hbm, q, ks, vs, outb, states_in, inverse, columns, rows, gain, sems,
):
    bad = jnp.max(flag[...]) > 0.0

    @pl.when(jnp.logical_not(bad))
    def _():
        pieces = [pl.ds(part * (T // 8), T // 8) for part in range(8)]
        arrive = [
            pltpu.make_async_copy(cand.at[piece], outb.at[piece], sems.at[part])
            for part, piece in enumerate(pieces)
        ]
        leave = [
            pltpu.make_async_copy(outb.at[piece], out_hbm.at[piece], sems.at[part])
            for part, piece in enumerate(pieces)
        ]
        for copy in arrive:
            copy.start()
        for there, onward in zip(arrive, leave):
            there.wait()
            onward.start()
        for copy in leave:
            copy.wait()

    @pl.when(bad)
    def _():
        def bring(source, target, sem):
            copy = pltpu.make_async_copy(source, target, sems.at[sem])
            copy.start()
            copy.wait()

        bring(q_hbm, q, 0)
        bring(states_hbm, states_in, 0)
        bring(inverse_hbm, inverse, 0)
        bring(columns_hbm, columns, 0)
        bring(rows_hbm, rows, 0)
        bring(gain_hbm, gain, 0)
        for head in range(KV):
            for source, whole, target in ((k_hbm, k_all, ks), (v_hbm, v_all, vs)):
                bring(source.at[:, pl.ds(head * H, H)], target.at[head, pl.ds(4 * T, T)], 0)
                for back in (1, 2, 3, 4):
                    bring(whole.at[back - 1, head], target.at[head, pl.ds((4 - back) * T, T)], 0)

        def query_step(index, carry):
            head = index // G
            at = head_columns(index)
            for first in range(0, T, 128):
                here = pl.ds(first, 128)
                queries = q[here, at]
                id_column, alive = columns[here, 4:5], columns[here, 5:6]
                before = columns[here, 6:7]
                spot = lax.broadcasted_iota(jnp.int32, (128, 5 * T), 1)
                turn = lax.broadcasted_iota(jnp.int32, (128, 5 * T), 0) + first
                inside = (spot > turn) & (spot <= turn + 4 * T)
                ids = jnp.concatenate([jnp.zeros((1, 4 * T), F32), rows[4:5, :]], 1)
                old = (alive > 0.0) & (spot.astype(F32) >= 4.0 * T - before)
                allowed = inside & (((spot < 4 * T) & old) | ((spot >= 4 * T) & (ids == id_column)))
                scores = nt(queries, ks[head]) * (1.0 / math.sqrt(HEAD_SIZE))
                scores = jnp.where(allowed, scores, HIDDEN)
                top = jnp.max(scores, axis=1, keepdims=True)
                grown = jnp.where(allowed, jnp.exp(scores - top), 0.0)
                weights = grown / jnp.sum(grown, axis=1, keepdims=True)
                window = nn(weights.astype(BF16), vs[head])
                row = rows[pl.ds(head, 1), :]
                lane = lax.broadcasted_iota(jnp.int32, (128, H), 1)
                column = jnp.sum(
                    jnp.where(lane == head, columns[here, :], 0.0), axis=1, keepdims=True
                )
                own_at = lax.broadcasted_iota(jnp.int32, (128, T), 1)
                own_turn = lax.broadcasted_iota(jnp.int32, (128, T), 0) + first
                linked = (own_at <= own_turn) & (rows[4:5, :] == id_column)
                gap = jnp.where(linked, column - row, 0.0)
                kept = jnp.where(linked, jnp.exp(gap), 0.0)
                dots = nt(queries, ks[head, pl.ds(4 * T, T)]) * kept
                linear = nn(dots.astype(BF16), vs[head, pl.ds(4 * T, T)])
                entry = jnp.exp(column) * alive
                linear = linear + nn(queries, states_in[head].astype(BF16)) * entry
                mixed = window + gain[:, at] * (linear * inverse[here, :])
                outb[here, at] = mixed.astype(BF16)
            return carry

        lax.fori_loop(0, KV * G, query_step, 0)
        bring(outb, out_hbm, 0)


def body(queries, keys, values, token_log_decay, seq_ids, norm_gain):
    any_spec = pl.BlockSpec(memory_space=pltpu.HBM)
    vmem_spec = pl.BlockSpec(memory_space=pltpu.VMEM)
    dma = pltpu.SemaphoreType.DMA
    gain = norm_gain.reshape(1, -1)
    ids = seq_ids.reshape(1, -1)
    wide = KV * G * H
    results = pl.pallas_call(
        main_kernel,
        out_shape=(
            jax.ShapeDtypeStruct((T, wide), BF16),
            jax.ShapeDtypeStruct((8, H), F32),
            jax.ShapeDtypeStruct((4, KV, T, H), BF16),
            jax.ShapeDtypeStruct((4, KV, T, H), BF16),
            jax.ShapeDtypeStruct((KV, H, H), F32),
            jax.ShapeDtypeStruct((T, H), F32),
            jax.ShapeDtypeStruct((T, H), F32),
            jax.ShapeDtypeStruct((8, T), F32),
        ),
        in_specs=[any_spec] * 3 + [vmem_spec] * 3,
        out_specs=(any_spec, vmem_spec, any_spec, any_spec, vmem_spec, vmem_spec, vmem_spec, vmem_spec),
        scratch_shapes=[
            pltpu.VMEM((T, wide), BF16),
            pltpu.VMEM((KV, T, H), BF16),
            pltpu.VMEM((KV, T, H), BF16),
            pltpu.VMEM((4, KV, T, H), BF16),
            pltpu.VMEM((4, KV, T, H), BF16),
            pltpu.VMEM((4, 1, T), jnp.int32),
            pltpu.VMEM((T, wide), F32),
            pltpu.VMEM((T, wide), F32),
            pltpu.VMEM((T, wide), F32),
            pltpu.VMEM((T, T), F32),
            pltpu.VMEM((T, T), F32),
            pltpu.VMEM((KV, T, H), F32),
            pltpu.VMEM((T, H), F32),
            pltpu.VMEM((T, H), F32),
            pltpu.VMEM((T, H), F32),
            pltpu.VMEM((4, STATE_ROWS, H), BF16),
            pltpu.VMEM((4, STATE_ROWS, H), BF16),
            pltpu.VMEM((4, STATE_ROWS, H), BF16),
            pltpu.VMEM((4, STATE_ROWS, H), BF16),
            pltpu.VMEM((4, H, H), BF16),
            pltpu.VMEM((4, H, H), BF16),
            pltpu.VMEM((STATE_ROWS, H), BF16),
            pltpu.VMEM((STATE_ROWS, H), BF16),
            pltpu.VMEM((T, wide), BF16),
            pltpu.VMEM((T, T), F32),
            pltpu.VMEM((2, T, H), BF16),
            pltpu.VMEM((2, T, H), BF16),
            dma((KV, 2)),
            dma,
            dma((KV,)),
            dma((4, KV, 2)),
            dma((4,)),
            dma((4,)),
            dma((4, KV, 2)),
            dma((4, KV, 2)),
            dma((4, 4)),
            dma((4, 4)),
            dma,
            dma,
            dma((2, 2)),
            dma((2, 2)),
        ],
        compiler_params=pltpu.CompilerParams(
            collective_id=0, has_side_effects=True, vmem_limit_bytes=56 << 20
        ),
        name="attend",
    )(queries, keys, values, token_log_decay, ids, gain)
    cand, flag, k_all, v_all, states_in, inverse, columns, rows = results
    return pl.pallas_call(
        finish_kernel,
        out_shape=jax.ShapeDtypeStruct((T, wide), BF16),
        in_specs=[vmem_spec] + [any_spec] * 11,
        out_specs=any_spec,
        scratch_shapes=[
            pltpu.VMEM((T, wide), BF16),
            pltpu.VMEM((KV, 5 * T, H), BF16),
            pltpu.VMEM((KV, 5 * T, H), BF16),
            pltpu.VMEM((T, wide), BF16),
            pltpu.VMEM((KV, H, H), F32),
            pltpu.VMEM((T, H), F32),
            pltpu.VMEM((T, H), F32),
            pltpu.VMEM((8, T), F32),
            pltpu.VMEM((1, wide), F32),
            dma((8,)),
        ],
        compiler_params=pltpu.CompilerParams(vmem_limit_bytes=56 << 20),
        name="finish",
    )(flag, cand, queries, keys, values, k_all, v_all, states_in, inverse, columns, rows, gain)


def solution(mesh):
    return jax.shard_map(
        body,
        mesh=mesh,
        in_specs=(
            P("ctx", "head"),
            P("ctx", "head"),
            P("ctx", "head"),
            P("head", "ctx"),
            P("ctx"),
            P("head"),
        ),
        out_specs=P("ctx", "head"),
        check_vma=False,
    )
```

```python
import math

import jax
import jax.numpy as jnp
from jax import lax
from jax.experimental import pallas as pl
from jax.experimental.pallas import tpu as pltpu
from jax.sharding import PartitionSpec as P

QUERY_HEADS = 32
KEY_VALUE_HEADS = 8
HEAD_SIZE = 128
WINDOW_LENGTH = 2048
LOG2E = 1.4426950408889634
SCALE = LOG2E / math.sqrt(HEAD_SIZE)
HIDDEN = -1e30
SMALL, LARGE = 2.0**-60, 2.0**110
MESH = pl.DeviceIdType.MESH
F32, BF16 = jnp.float32, jnp.bfloat16
T = 512
H = HEAD_SIZE
KV = 4
G = 4
STATE_ROWS = H + 16
ORDERS = (
    ((1, 0), (3, 2), (3, 3), (1, 1), (3, 0), (2, 0), (2, 2), (2, 1), (1, 2), (3, 1), (1, 3), (2, 3)),
    ((1, 0), (1, 1), (3, 2), (1, 2), (3, 3), (1, 3), (3, 0), (3, 1), (2, 0), (2, 1), (2, 2), (2, 3)),
    ((1, 0), (1, 1), (3, 0), (1, 2), (3, 1), (3, 2), (1, 3), (3, 3), (2, 0), (2, 1), (2, 2), (2, 3)),
    ((1, 0), (3, 2), (1, 1), (3, 3), (1, 2), (3, 0), (1, 3), (3, 1), (2, 0), (2, 1), (2, 2), (2, 3)),
)


def nt(a, b):
    return lax.dot_general(a, b, (((1,), (1,)), ((), ())), preferred_element_type=F32)


def nn(a, b):
    return lax.dot_general(a, b, (((1,), (0,)), ((), ())), preferred_element_type=F32)


def tn(a, b):
    return lax.dot_general(a, b, (((0,), (0,)), ((), ())), preferred_element_type=F32)


def pack_state(state, factor):
    high = factor.astype(BF16).astype(F32)
    middle = (factor - high).astype(BF16).astype(F32)
    low = factor - high - middle
    row = lax.broadcasted_iota(jnp.int32, (16, H), 0)
    tail = jnp.where(row < 4, high, jnp.where(row < 8, middle, low))
    return jnp.concatenate([state, tail], 0).astype(BF16)


def unpack_state(message):
    tail = message[H:, :].astype(F32)
    return message[:H, :].astype(F32), tail[0:1] + tail[4:5] + tail[8:9]


def head_columns(index):
    return pl.ds(pl.multiple_of(index * H, H), H)


def main_kernel(
    q_hbm, k_hbm, v_hbm, decay, ids, gain,
    out_hbm, flag, k_all, v_all, states_in, inverse_out, columns_out, rows_out,
    q, kb, vb, rk, rv, rid, acc, total, lin, causal, later, cum, alive_ref, squares, partner,
    sa, ra, rx, ry, sd, rd, sx, sy, outb, own_decay,
    sk, sv,
    in_sem, q_sem, out_sem, save_sem, ids_s, ids_r, block_s, block_r,
    st_s, st_r, sq_s, sq_r, stop_s, stop_r,
):
    me = lax.axis_index("ctx")
    core = lax.axis_index("head")
    z = lax.rem(me, 4)
    x = lax.rem(me // 4, 4)
    y = me // 16
    line = me - z

    def dev(ctx):
        return {"ctx": ctx, "head": core}

    def around(offset):
        return lax.rem(me + (offset + 64), 64)

    def on_line(position):
        return line + position

    def on_x(position):
        return y * 16 + position * 4 + z

    def on_y(position):
        return position * 16 + x * 4 + z

    def own_chunk(head, kind):
        source, target = ((k_hbm, kb), (v_hbm, vb))[kind]
        return pltpu.make_async_copy(
            source.at[:, pl.ds(head * H, H)], target.at[head], in_sem.at[head, kind]
        )

    chunk_order = (2, 0, 3, 1)
    for head in chunk_order:
        own_chunk(head, 0).start()
        own_chunk(head, 1).start()
    q_copy = pltpu.make_async_copy(q_hbm, q, q_sem)
    q_copy.start()

    barrier = pltpu.get_barrier_semaphore()
    for offset in (1, 2, 3, 4, -1, -2, -3, -4):
        pl.semaphore_signal(barrier, inc=1, device_id=dev(around(offset)), device_id_type=MESH)
    for step in (1, 2, 3):
        for ctx in (
            on_line(lax.rem(z + step, 4)),
            on_x(lax.rem(x + step, 4)),
            on_y(lax.rem(y + step, 4)),
        ):
            pl.semaphore_signal(barrier, inc=1, device_id=dev(ctx), device_id_type=MESH)
    other = {"ctx": me, "head": 1 - core}
    pl.semaphore_signal(barrier, inc=1, device_id=other, device_id_type=MESH)
    pl.semaphore_wait(barrier, 18)

    def id_copy(back):
        return pltpu.make_async_remote_copy(
            src_ref=ids, dst_ref=rid.at[back - 1], send_sem=ids_s.at[back - 1],
            recv_sem=ids_r.at[back - 1], device_id=dev(around(back)), device_id_type=MESH,
        )

    for back in (1, 2, 3, 4):
        id_copy(back).start()

    to_four = around(4)
    to_one = jnp.where(z < 3, around(1), on_line(0))
    to_three = jnp.where(z > 0, around(-1), on_line(3))

    def block_copy(source, back, head, kind, target):
        return pltpu.make_async_remote_copy(
            src_ref=source, dst_ref=(rk, rv)[kind].at[back - 1, head],
            send_sem=block_s.at[back - 1, head, kind], recv_sem=block_r.at[back - 1, head, kind],
            device_id=dev(target), device_id_type=MESH,
        )

    first_early = jnp.where(z < 3, 2, 0)

    def early_head(step):
        return lax.rem(first_early + step, 4)

    def own_send(step, kind):
        early, late = early_head(step), step
        block_copy((kb, vb)[kind].at[early], 4, early, kind, to_four).start()

        @pl.when(z < 3)
        def _():
            block_copy((kb, vb)[kind].at[late], 1, late, kind, to_one).start()

        @pl.when(z == 0)
        def _():
            block_copy((kb, vb)[kind].at[early], 3, early, kind, to_three).start()

    def receive(back, head):
        for kind in (0, 1):
            block_copy((kb, vb)[kind].at[head], back, head, kind, to_four).wait_recv()

    def save_one(back, head, kind):
        pltpu.make_async_copy(
            (rk, rv)[kind].at[back - 1, head], (k_all, v_all)[kind].at[back - 1, head],
            save_sem.at[back - 1, head, kind],
        ).start()

    def save(back, head):
        for kind in (0, 1):
            save_one(back, head, kind)

    def relay_four(step, kind, up=True, down=True):
        head = early_head(step)
        held = (rk, rv)[kind].at[3, head]
        if down:
            block_copy(held, 4, head, kind, to_four).wait_recv()
        if up:

            @pl.when(z == 3)
            def _():
                block_copy(held, 1, head, kind, to_one).start()

        if down:

            @pl.when(z > 0)
            def _():
                block_copy(held, 3, head, kind, to_three).start()

            save_one(4, head, kind)

    def stop_copy(source, head, kind, target):
        slot = lax.rem(head, 2)
        return pltpu.make_async_remote_copy(
            src_ref=source, dst_ref=(sk, sv)[kind].at[slot],
            send_sem=block_s.at[1, head, kind], recv_sem=stop_r.at[slot, kind],
            device_id=dev(target), device_id_type=MESH,
        )

    def relay_up(head):
        for kind in (0, 1):
            held = (rk, rv)[kind].at[0, head]

            @pl.when(z < 3)
            def _():
                block_copy(held, 2, head, kind, around(1)).start()

            @pl.when(z == 3)
            def _():
                stop_copy(held, head, kind, on_line(0)).start()

    def relay_down(head):
        for kind in (0, 1):
            held = (rk, rv)[kind].at[2, head]

            @pl.when(z > 0)
            def _():
                block_copy(held, 2, head, kind, around(-1)).start()

            @pl.when(z == 0)
            def _():
                stop_copy(held, head, kind, on_line(3)).start()

    onward_line = jnp.where(z == 0, around(4), around(-4))
    onward_first = jnp.where(z == 0, 0, 2)

    def onward_copy(slot, kind):
        head = onward_first + slot
        return pltpu.make_async_remote_copy(
            src_ref=(sk, sv)[kind].at[slot], dst_ref=(rk, rv)[kind].at[1, head],
            send_sem=stop_s.at[slot, kind], recv_sem=block_r.at[1, head, kind],
            device_id=dev(onward_line), device_id_type=MESH,
        )

    def hand_on(slot, at):
        @pl.when(z == at)
        def _():
            for kind in (0, 1):
                stop_copy((sk, sv)[kind].at[slot], slot, kind, on_line(0)).wait_recv()
                onward_copy(slot, kind).start()

    for head in chunk_order:
        own_chunk(head, 0).wait()
        own_chunk(head, 1).wait()
        if head == 0:
            own_send(0, 0)
            own_send(0, 1)
    own_send(1, 0)

    running = decay[...]
    shift = 1
    lane = lax.broadcasted_iota(jnp.int32, (KV, T), 1)
    while shift < T:
        running = running + jnp.where(lane >= shift, pltpu.roll(running, shift, 1), 0.0)
        shift *= 2
    id_row = ids[...].astype(F32)
    rows = jnp.concatenate([running, id_row, jnp.zeros((3, T), F32)], 0)
    rows_out[...] = rows
    columns = jnp.concatenate([rows, jnp.zeros((H - 8, T), F32)], 0).T
    id_column = jnp.broadcast_to(columns[:, 4:5], (T, H))
    for head in range(KV):
        cum[head] = jnp.broadcast_to(columns[:, head : head + 1], (T, H))
    for part in range(4):
        row_at = lax.broadcasted_iota(jnp.int32, (T, H), 0)
        column_at = lax.broadcasted_iota(jnp.int32, (T, H), 1) + part * H
        span = slice(part * H, (part + 1) * H)
        linked = (column_at <= row_at) & (id_column == id_row[:, span])
        causal[:, span] = jnp.where(linked, 0.0, HIDDEN)
        later[:, span] = jnp.where(column_at > row_at, 0.0, HIDDEN)
    last_id = id_row[:, T - 1 : T]
    own_tail = id_column == last_id

    relay_four(0, 0)
    for back in (1, 2, 3, 4):
        id_copy(back).wait_recv()
    prev_id = jnp.where(me > 0, rid[0].astype(F32)[:, T - 1 : T], -1.0)
    before = jnp.zeros((1, 1), F32)
    for back in (1, 2, 3, 4):
        same = (rid[back - 1].astype(F32) == prev_id).astype(F32)
        count = jnp.sum(same, axis=1, keepdims=True)
        before = before + jnp.where(me >= back, count, 0.0)
    alive = (id_column == prev_id).astype(F32)
    alive_ref[...] = alive
    lane_at = lax.broadcasted_iota(jnp.int32, (T, H), 1)
    columns_out[...] = jnp.where(
        lane_at == 5, alive, jnp.where(lane_at == 6, jnp.broadcast_to(before, (T, H)), columns)
    )
    own_carry = (last_id == prev_id).astype(F32)

    for head in range(KV):
        end = running[head : head + 1, T - 1 : T]
        weight = jnp.where(own_tail, jnp.exp(end - cum[head]), 0.0)
        weighted = (kb[head].astype(F32) * weight).astype(BF16)
        state = tn(weighted, vb[head])
        factor = jnp.broadcast_to(jnp.exp(end) * own_carry, (1, H))
        sa[head] = pack_state(state, factor)

    def state_copy(stage, source, target, slot, ctx):
        return pltpu.make_async_remote_copy(
            src_ref=source, dst_ref=target.at[slot], send_sem=st_s.at[stage, slot],
            recv_sem=st_r.at[stage, slot], device_id=dev(ctx), device_id_type=MESH,
        )

    def state_send(stage, step):
        if stage == 0:
            to = lax.rem(z + step, 4)
            return pltpu.make_async_remote_copy(
                src_ref=sa.at[to], dst_ref=ra.at[z], send_sem=st_s.at[0, step], recv_sem=st_r.at[0, step],
                device_id=dev(on_line(to)), device_id_type=MESH,
            )
        if stage == 1:
            return pltpu.make_async_remote_copy(
                src_ref=sx, dst_ref=rx.at[x], send_sem=st_s.at[1, step], recv_sem=st_r.at[1, step],
                device_id=dev(on_x(lax.rem(x + step, 4))), device_id_type=MESH,
            )
        if stage == 2:
            return pltpu.make_async_remote_copy(
                src_ref=sy, dst_ref=ry.at[y], send_sem=st_s.at[2, step], recv_sem=st_r.at[2, step],
                device_id=dev(on_y(lax.rem(y + step, 4))), device_id_type=MESH,
            )
        to = lax.rem(z + step, 4)
        return pltpu.make_async_remote_copy(
            src_ref=sd.at[to], dst_ref=rd.at[z], send_sem=st_s.at[3, step], recv_sem=st_r.at[3, step],
            device_id=dev(on_line(to)), device_id_type=MESH,
        )

    def start_stage(stage):
        for step in (1, 2, 3):
            state_send(stage, step).start()

    def finish_stage(stage):
        for step in (1, 2, 3):
            state_send(stage, step).wait_recv()

    ra[z] = sa[z]
    start_stage(0)

    def fold(messages, limit=None):
        state, factor = jnp.zeros((H, H), F32), jnp.ones((1, H), F32)
        for position in range(4):
            item, by = unpack_state(messages[position])
            fresh, grown = state * by + item, factor * by
            if limit is None:
                state, factor = fresh, grown
            else:
                state = jnp.where(position < limit, fresh, state)
        return state, factor

    def after_line():
        finish_stage(0)
        sx[...] = pack_state(*fold(ra))
        rx[x] = sx[...]
        start_stage(1)

    def after_x():
        finish_stage(1)
        sy[...] = pack_state(*fold(rx))
        ry[y] = sy[...]
        start_stage(2)

    def after_y():
        finish_stage(2)
        state, _ = fold(ry, y)
        for position in range(4):
            item, by = unpack_state(rx[position])
            state = jnp.where(position < x, state * by + item, state)
        for position in range(4):
            sd[position] = state.astype(BF16)
            item, by = unpack_state(ra[position])
            state = state * by + item
        rd[z] = sd[z]
        start_stage(3)

    q_copy.wait()

    def own_unit(head):
        keys, values = kb[head], vb[head]
        wide = jnp.concatenate([values, jnp.ones((T, H), BF16)], 1)
        row = rows_out[pl.ds(head, 1), :]
        for first in (0, 256):
            here, upto = slice(first, first + 256), first + 256
            column = cum[head, here, :]
            for part in range(0, upto, H):
                span = slice(part, part + H)
                own_decay[here, span] = jnp.exp(column - row[:, span] + causal[here, span])
        for first in (0, 256):
            here, upto = slice(first, first + 256), first + 256
            for member in range(G):
                at = head_columns(head * G + member)
                scores = nt(q[here, at], keys[:upto])
                grown = jnp.exp2(scores * SCALE + causal[here, :upto]).astype(BF16)
                mixed = nn(grown, wide[:upto])
                acc[here, at] = mixed[:, :H]
                total[here, at] = mixed[:, H:]
                lin[here, at] = nn((scores * own_decay[here, :upto]).astype(BF16), values[:upto])

    def masked_values(back, head):
        place = lax.broadcasted_iota(jnp.int32, (T, H), 0).astype(F32)
        kept = place >= back * float(T) - columns_out[0:1, 6:7]
        values = jnp.where(kept, rv[back - 1, head].astype(F32), 0.0)
        return jnp.concatenate([values, jnp.where(kept, 1.0, 0.0)], 1).astype(BF16)

    def gather(here, at, mixed):
        live = alive_ref[here, :] > 0.0
        acc[here, at] += jnp.where(live, mixed[:, :H], 0.0)
        total[here, at] += jnp.where(live, mixed[:, H:], 0.0)

    def far_unit(back, head):
        keys, wide = rk[back - 1, head], masked_values(back, head)
        for member in range(G):
            at = head_columns(head * G + member)
            grown = jnp.exp2(nt(q[:, at], keys) * SCALE).astype(BF16)
            gather(slice(0, T), at, nn(grown, wide))

    def oldest_unit(head):
        keys, wide = rk[3, head], masked_values(4, head)
        for first in (0, 256):
            here, since = slice(first, first + 256), slice(first, T)
            for member in range(G):
                at = head_columns(head * G + member)
                scores = nt(q[here, at], keys[since])
                grown = jnp.exp2(scores * SCALE + later[here, since]).astype(BF16)
                gather(here, at, nn(grown, wide[since]))

    relay_four(0, 1)
    own_send(1, 1)

    def first_up(head, at_end):
        @pl.when((z == 3) == at_end)
        def _():
            receive(1, head)
            relay_up(head)
            save(1, head)

    def own_step(head, carry):
        own_unit(head)

        @pl.when(head == 0)
        def _():
            own_send(2, 0)

        @pl.when(head == 1)
        def _():
            after_line()
            own_send(2, 1)
            first_up(0, True)

        @pl.when(head == 2)
        def _():
            relay_four(1, 0)
            relay_four(1, 1)
            own_send(3, 0)

        @pl.when(head == 3)
        def _():
            own_send(3, 1)
            first_up(0, False)
            first_up(1, True)

        return carry

    lax.fori_loop(0, KV, own_step, 0)

    def cross():
        finish_stage(3)
        squares[...] = jnp.zeros((T, H), F32)

        def cross_step(head, carry):
            state = rd[head]
            states_in[head] = state.astype(F32)
            entry = jnp.exp(cum[head]) * alive_ref[...]
            part = squares[...]
            for member in range(G):
                at = head_columns(head * G + member)
                whole = lin[:, at] + nn(q[:, at], state) * entry
                lin[:, at] = whole
                part = part + whole * whole
            squares[...] = part
            return carry

        lax.fori_loop(0, KV, cross_step, 0)
        row_sum = jnp.sum(squares[...], axis=1, keepdims=True)
        squares[...] = jnp.broadcast_to(row_sum, (T, H))
        square_copy().start()

    def square_copy():
        return pltpu.make_async_remote_copy(
            src_ref=squares, dst_ref=partner, send_sem=sq_s, recv_sem=sq_r, device_id=other,
            device_id_type=MESH,
        )

    def out_copy(head):
        wide = pl.ds(pl.multiple_of(head * G * H, G * H), G * H)
        return pltpu.make_async_copy(outb.at[:, wide], out_hbm.at[:, wide], out_sem.at[head])

    def listed(step):
        code = jnp.int32(0)
        for place, order in enumerate(ORDERS):
            mine = jnp.int32(0)
            for index, (back, head) in enumerate(order):
                mine = jnp.where(step == index, back * 4 + head, mine)
            code = jnp.where(z == place, mine, code)
        return code // 4, lax.rem(code, 4)

    def far_step(step, carry):
        back, head = listed(step)

        @pl.when(step == 1)
        def _():
            after_x()

        @pl.when(step == 3)
        def _():
            after_y()

        @pl.when(step == 1)
        def _():
            relay_four(2, 0, up=False)
            relay_four(2, 1, up=False)

        @pl.when(step == 2)
        def _():
            relay_four(2, 0, down=False)
            relay_four(2, 1, down=False)
            hand_on(0, 0)

        @pl.when(step == 3)
        def _():
            relay_four(3, 0)
            relay_four(3, 1)

        @pl.when(step == 6)
        def _():
            hand_on(1, 0)
            hand_on(0, 3)

        @pl.when(step == 7)
        def _():
            cross()

        @pl.when(step == 8)
        def _():
            hand_on(1, 3)
            square_copy().wait_recv()
            mean = (squares[...] + partner[...]) * (1.0 / (QUERY_HEADS * HEAD_SIZE))
            inverse_out[...] = lax.rsqrt(mean + 1e-06)
            flag[...] = jnp.zeros((8, H), F32)

        @pl.when((back != 1) | (head > jnp.where(z == 3, 1, 0)))
        def _():
            receive(back, head)
            save(back, head)

        @pl.when((back == 1) & (head == 1) & (z < 3))
        def _():
            relay_up(head)

        @pl.when((back == 3) & (head >= 2))
        def _():
            relay_down(head)

        far_unit(back, head)
        return carry

    def old_step(step, carry):
        oldest_unit(early_head(step))
        lax.fori_loop(2 * step, 2 * step + 2, far_step, 0)
        return carry

    def last_step(step, carry):
        far_step(step, carry)
        head = step - 8
        head = jnp.where((z == 0) & (head > 0) & (head < 3), 3 - head, head)
        for member in range(G):
            at = head_columns(head * G + member)
            mass = total[:, at]
            good = (mass >= SMALL) & (mass <= LARGE)
            flag[...] += jnp.sum(jnp.where(good, 0.0, 1.0).reshape(T // 8, 8, H), axis=0)
            mixed = acc[:, at] / mass + gain[:, at] * (lin[:, at] * inverse_out[...])
            outb[:, at] = mixed.astype(BF16)
        out_copy(head).start()
        return carry

    lax.fori_loop(0, 4, old_step, 0)
    lax.fori_loop(8, 12, last_step, 0)

    for head in range(KV):
        out_copy(head).wait()
        for kind in (0, 1):
            for back in (1, 2, 3, 4):
                held = (rk, rv)[kind].at[back - 1, head]
                pltpu.make_async_copy(
                    held, (k_all, v_all)[kind].at[back - 1, head], save_sem.at[back - 1, head, kind]
                ).wait()
                block_copy(held, back, head, kind, to_four).wait_send()
    for back in (1, 2, 3, 4):
        id_copy(back).wait_send()
    for stage in range(4):
        for step in (1, 2, 3):
            state_send(stage, step).wait_send()
    square_copy().wait_send()

    @pl.when((z == 0) | (z == 3))
    def _():
        for slot in (0, 1):
            for kind in (0, 1):
                onward_copy(slot, kind).wait_send()


def finish_kernel(
    flag, cand, q_hbm, k_hbm, v_hbm, k_all, v_all, states_hbm, inverse_hbm, columns_hbm, rows_hbm, gain_hbm,
    out_hbm, q, ks, vs, outb, states_in, inverse, columns, rows, gain, sems,
):
    bad = jnp.max(flag[...]) > 0.0

    @pl.when(jnp.logical_not(bad))
    def _():
        pieces = [pl.ds(part * (T // 8), T // 8) for part in range(8)]
        arrive = [
            pltpu.make_async_copy(cand.at[piece], outb.at[piece], sems.at[part])
            for part, piece in enumerate(pieces)
        ]
        leave = [
            pltpu.make_async_copy(outb.at[piece], out_hbm.at[piece], sems.at[part])
            for part, piece in enumerate(pieces)
        ]
        for copy in arrive:
            copy.start()
        for there, onward in zip(arrive, leave):
            there.wait()
            onward.start()
        for copy in leave:
            copy.wait()

    @pl.when(bad)
    def _():
        def bring(source, target, sem):
            copy = pltpu.make_async_copy(source, target, sems.at[sem])
            copy.start()
            copy.wait()

        bring(q_hbm, q, 0)
        bring(states_hbm, states_in, 0)
        bring(inverse_hbm, inverse, 0)
        bring(columns_hbm, columns, 0)
        bring(rows_hbm, rows, 0)
        bring(gain_hbm, gain, 0)
        for head in range(KV):
            for source, whole, target in ((k_hbm, k_all, ks), (v_hbm, v_all, vs)):
                bring(source.at[:, pl.ds(head * H, H)], target.at[head, pl.ds(4 * T, T)], 0)
                for back in (1, 2, 3, 4):
                    bring(whole.at[back - 1, head], target.at[head, pl.ds((4 - back) * T, T)], 0)

        def query_step(index, carry):
            head = index // G
            at = head_columns(index)
            for first in range(0, T, 128):
                here = pl.ds(first, 128)
                queries = q[here, at]
                id_column, alive = columns[here, 4:5], columns[here, 5:6]
                before = columns[here, 6:7]
                spot = lax.broadcasted_iota(jnp.int32, (128, 5 * T), 1)
                turn = lax.broadcasted_iota(jnp.int32, (128, 5 * T), 0) + first
                inside = (spot > turn) & (spot <= turn + 4 * T)
                ids = jnp.concatenate([jnp.zeros((1, 4 * T), F32), rows[4:5, :]], 1)
                old = (alive > 0.0) & (spot.astype(F32) >= 4.0 * T - before)
                allowed = inside & (((spot < 4 * T) & old) | ((spot >= 4 * T) & (ids == id_column)))
                scores = nt(queries, ks[head]) * (1.0 / math.sqrt(HEAD_SIZE))
                scores = jnp.where(allowed, scores, HIDDEN)
                top = jnp.max(scores, axis=1, keepdims=True)
                grown = jnp.where(allowed, jnp.exp(scores - top), 0.0)
                weights = grown / jnp.sum(grown, axis=1, keepdims=True)
                window = nn(weights.astype(BF16), vs[head])
                row = rows[pl.ds(head, 1), :]
                lane = lax.broadcasted_iota(jnp.int32, (128, H), 1)
                column = jnp.sum(
                    jnp.where(lane == head, columns[here, :], 0.0), axis=1, keepdims=True
                )
                own_at = lax.broadcasted_iota(jnp.int32, (128, T), 1)
                own_turn = lax.broadcasted_iota(jnp.int32, (128, T), 0) + first
                linked = (own_at <= own_turn) & (rows[4:5, :] == id_column)
                gap = jnp.where(linked, column - row, 0.0)
                kept = jnp.where(linked, jnp.exp(gap), 0.0)
                dots = nt(queries, ks[head, pl.ds(4 * T, T)]) * kept
                linear = nn(dots.astype(BF16), vs[head, pl.ds(4 * T, T)])
                entry = jnp.exp(column) * alive
                linear = linear + nn(queries, states_in[head].astype(BF16)) * entry
                mixed = window + gain[:, at] * (linear * inverse[here, :])
                outb[here, at] = mixed.astype(BF16)
            return carry

        lax.fori_loop(0, KV * G, query_step, 0)
        bring(outb, out_hbm, 0)


def body(queries, keys, values, token_log_decay, seq_ids, norm_gain):
    any_spec = pl.BlockSpec(memory_space=pltpu.HBM)
    vmem_spec = pl.BlockSpec(memory_space=pltpu.VMEM)
    dma = pltpu.SemaphoreType.DMA
    gain = norm_gain.reshape(1, -1)
    ids = seq_ids.reshape(1, -1)
    wide = KV * G * H
    results = pl.pallas_call(
        main_kernel,
        out_shape=(
            jax.ShapeDtypeStruct((T, wide), BF16),
            jax.ShapeDtypeStruct((8, H), F32),
            jax.ShapeDtypeStruct((4, KV, T, H), BF16),
            jax.ShapeDtypeStruct((4, KV, T, H), BF16),
            jax.ShapeDtypeStruct((KV, H, H), F32),
            jax.ShapeDtypeStruct((T, H), F32),
            jax.ShapeDtypeStruct((T, H), F32),
            jax.ShapeDtypeStruct((8, T), F32),
        ),
        in_specs=[any_spec] * 3 + [vmem_spec] * 3,
        out_specs=(any_spec, vmem_spec, any_spec, any_spec, vmem_spec, vmem_spec, vmem_spec, vmem_spec),
        scratch_shapes=[
            pltpu.VMEM((T, wide), BF16),
            pltpu.VMEM((KV, T, H), BF16),
            pltpu.VMEM((KV, T, H), BF16),
            pltpu.VMEM((4, KV, T, H), BF16),
            pltpu.VMEM((4, KV, T, H), BF16),
            pltpu.VMEM((4, 1, T), jnp.int32),
            pltpu.VMEM((T, wide), F32),
            pltpu.VMEM((T, wide), F32),
            pltpu.VMEM((T, wide), F32),
            pltpu.VMEM((T, T), F32),
            pltpu.VMEM((T, T), F32),
            pltpu.VMEM((KV, T, H), F32),
            pltpu.VMEM((T, H), F32),
            pltpu.VMEM((T, H), F32),
            pltpu.VMEM((T, H), F32),
            pltpu.VMEM((4, STATE_ROWS, H), BF16),
            pltpu.VMEM((4, STATE_ROWS, H), BF16),
            pltpu.VMEM((4, STATE_ROWS, H), BF16),
            pltpu.VMEM((4, STATE_ROWS, H), BF16),
            pltpu.VMEM((4, H, H), BF16),
            pltpu.VMEM((4, H, H), BF16),
            pltpu.VMEM((STATE_ROWS, H), BF16),
            pltpu.VMEM((STATE_ROWS, H), BF16),
            pltpu.VMEM((T, wide), BF16),
            pltpu.VMEM((T, T), F32),
            pltpu.VMEM((2, T, H), BF16),
            pltpu.VMEM((2, T, H), BF16),
            dma((KV, 2)),
            dma,
            dma((KV,)),
            dma((4, KV, 2)),
            dma((4,)),
            dma((4,)),
            dma((4, KV, 2)),
            dma((4, KV, 2)),
            dma((4, 4)),
            dma((4, 4)),
            dma,
            dma,
            dma((2, 2)),
            dma((2, 2)),
        ],
        compiler_params=pltpu.CompilerParams(
            collective_id=0, has_side_effects=True, vmem_limit_bytes=56 << 20
        ),
        name="attend",
    )(queries, keys, values, token_log_decay, ids, gain)
    cand, flag, k_all, v_all, states_in, inverse, columns, rows = results
    return pl.pallas_call(
        finish_kernel,
        out_shape=jax.ShapeDtypeStruct((T, wide), BF16),
        in_specs=[vmem_spec] + [any_spec] * 11,
        out_specs=any_spec,
        scratch_shapes=[
            pltpu.VMEM((T, wide), BF16),
            pltpu.VMEM((KV, 5 * T, H), BF16),
            pltpu.VMEM((KV, 5 * T, H), BF16),
            pltpu.VMEM((T, wide), BF16),
            pltpu.VMEM((KV, H, H), F32),
            pltpu.VMEM((T, H), F32),
            pltpu.VMEM((T, H), F32),
            pltpu.VMEM((8, T), F32),
            pltpu.VMEM((1, wide), F32),
            dma((8,)),
        ],
        compiler_params=pltpu.CompilerParams(vmem_limit_bytes=56 << 20),
        name="finish",
    )(flag, cand, queries, keys, values, k_all, v_all, states_in, inverse, columns, rows, gain)


def solution(mesh):
    return jax.shard_map(
        body,
        mesh=mesh,
        in_specs=(
            P("ctx", "head"),
            P("ctx", "head"),
            P("ctx", "head"),
            P("head", "ctx"),
            P("ctx"),
            P("head"),
        ),
        out_specs=P("ctx", "head"),
        check_vma=False,
    )
```

```python
import math

import jax
import jax.numpy as jnp
from jax import lax
from jax.experimental import pallas as pl
from jax.experimental.pallas import tpu as pltpu
from jax.sharding import PartitionSpec as P

QUERY_HEADS = 32
KEY_VALUE_HEADS = 8
HEAD_SIZE = 128
WINDOW_LENGTH = 2048
LOG2E = 1.4426950408889634
SCALE = LOG2E / math.sqrt(HEAD_SIZE)
HIDDEN = -1e30
SMALL, LARGE = 2.0**-60, 2.0**110
MESH = pl.DeviceIdType.MESH
F32, BF16 = jnp.float32, jnp.bfloat16
T = 512
H = HEAD_SIZE
KV = 4
G = 4
STATE_ROWS = H + 16
ORDERS = (
    ((1, 0), (3, 2), (3, 3), (1, 1), (3, 0), (2, 0), (3, 1), (2, 2), (1, 2), (2, 1), (1, 3), (2, 3)),
    ((1, 0), (1, 1), (3, 2), (1, 2), (3, 3), (1, 3), (3, 0), (3, 1), (2, 0), (2, 1), (2, 2), (2, 3)),
    ((1, 0), (1, 1), (3, 0), (1, 2), (3, 1), (3, 2), (1, 3), (3, 3), (2, 0), (2, 1), (2, 2), (2, 3)),
    ((1, 0), (3, 2), (1, 1), (3, 3), (1, 2), (3, 0), (1, 3), (3, 1), (2, 0), (2, 1), (2, 2), (2, 3)),
)


def nt(a, b):
    return lax.dot_general(a, b, (((1,), (1,)), ((), ())), preferred_element_type=F32)


def nn(a, b):
    return lax.dot_general(a, b, (((1,), (0,)), ((), ())), preferred_element_type=F32)


def tn(a, b):
    return lax.dot_general(a, b, (((0,), (0,)), ((), ())), preferred_element_type=F32)


def pack_state(state, factor):
    high = factor.astype(BF16).astype(F32)
    middle = (factor - high).astype(BF16).astype(F32)
    low = factor - high - middle
    row = lax.broadcasted_iota(jnp.int32, (16, H), 0)
    tail = jnp.where(row < 4, high, jnp.where(row < 8, middle, low))
    return jnp.concatenate([state, tail], 0).astype(BF16)


def unpack_state(message):
    tail = message[H:, :].astype(F32)
    return message[:H, :].astype(F32), tail[0:1] + tail[4:5] + tail[8:9]


def head_columns(index):
    return pl.ds(pl.multiple_of(index * H, H), H)


def main_kernel(
    q_hbm, k_hbm, v_hbm, decay, ids, gain,
    out_hbm, flag, k_all, v_all, states_in, inverse_out, columns_out, rows_out,
    q, kb, vb, rk, rv, rid, acc, total, lin, causal, later, cum, alive_ref, squares, partner,
    sa, ra, rx, ry, sd, rd, sx, sy, outb, own_decay,
    sk, sv,
    in_sem, q_sem, out_sem, save_sem, ids_s, ids_r, block_s, block_r,
    st_s, st_r, sq_s, sq_r, stop_s, stop_r,
):
    me = lax.axis_index("ctx")
    core = lax.axis_index("head")
    z = lax.rem(me, 4)
    x = lax.rem(me // 4, 4)
    y = me // 16
    line = me - z

    def dev(ctx):
        return {"ctx": ctx, "head": core}

    def around(offset):
        return lax.rem(me + (offset + 64), 64)

    def on_line(position):
        return line + position

    def on_x(position):
        return y * 16 + position * 4 + z

    def on_y(position):
        return position * 16 + x * 4 + z

    def own_chunk(head, kind):
        source, target = ((k_hbm, kb), (v_hbm, vb))[kind]
        return pltpu.make_async_copy(
            source.at[:, pl.ds(head * H, H)], target.at[head], in_sem.at[head, kind]
        )

    chunk_order = (2, 0, 3, 1)
    for head in chunk_order:
        own_chunk(head, 0).start()
        own_chunk(head, 1).start()
    q_copy = pltpu.make_async_copy(q_hbm, q, q_sem)
    q_copy.start()

    barrier = pltpu.get_barrier_semaphore()
    for offset in (1, 2, 3, 4, -1, -2, -3, -4):
        pl.semaphore_signal(barrier, inc=1, device_id=dev(around(offset)), device_id_type=MESH)
    for step in (1, 2, 3):
        for ctx in (
            on_line(lax.rem(z + step, 4)),
            on_x(lax.rem(x + step, 4)),
            on_y(lax.rem(y + step, 4)),
        ):
            pl.semaphore_signal(barrier, inc=1, device_id=dev(ctx), device_id_type=MESH)
    other = {"ctx": me, "head": 1 - core}
    pl.semaphore_signal(barrier, inc=1, device_id=other, device_id_type=MESH)
    pl.semaphore_wait(barrier, 18)

    def id_copy(back):
        return pltpu.make_async_remote_copy(
            src_ref=ids, dst_ref=rid.at[back - 1], send_sem=ids_s.at[back - 1],
            recv_sem=ids_r.at[back - 1], device_id=dev(around(back)), device_id_type=MESH,
        )

    for back in (1, 2, 3, 4):
        id_copy(back).start()

    to_four = around(4)
    to_one = jnp.where(z < 3, around(1), on_line(0))
    to_three = jnp.where(z > 0, around(-1), on_line(3))

    def block_copy(source, back, head, kind, target):
        return pltpu.make_async_remote_copy(
            src_ref=source, dst_ref=(rk, rv)[kind].at[back - 1, head],
            send_sem=block_s.at[back - 1, head, kind], recv_sem=block_r.at[back - 1, head, kind],
            device_id=dev(target), device_id_type=MESH,
        )

    first_early = jnp.where(z < 3, 2, 0)

    def early_head(step):
        return lax.rem(first_early + step, 4)

    def own_send(step, kind):
        early, late = early_head(step), step
        block_copy((kb, vb)[kind].at[early], 4, early, kind, to_four).start()

        @pl.when(z < 3)
        def _():
            block_copy((kb, vb)[kind].at[late], 1, late, kind, to_one).start()

        @pl.when(z == 0)
        def _():
            block_copy((kb, vb)[kind].at[early], 3, early, kind, to_three).start()

    def receive(back, head):
        for kind in (0, 1):
            block_copy((kb, vb)[kind].at[head], back, head, kind, to_four).wait_recv()

    def save_one(back, head, kind):
        pltpu.make_async_copy(
            (rk, rv)[kind].at[back - 1, head], (k_all, v_all)[kind].at[back - 1, head],
            save_sem.at[back - 1, head, kind],
        ).start()

    def save(back, head):
        for kind in (0, 1):
            save_one(back, head, kind)

    def relay_four(step, kind, up=True, down=True):
        head = early_head(step)
        held = (rk, rv)[kind].at[3, head]
        if down:
            block_copy(held, 4, head, kind, to_four).wait_recv()
        if up:

            @pl.when(z == 3)
            def _():
                block_copy(held, 1, head, kind, to_one).start()

        if down:

            @pl.when(z > 0)
            def _():
                block_copy(held, 3, head, kind, to_three).start()

            save_one(4, head, kind)

    def stop_copy(source, head, kind, target):
        slot = lax.rem(head, 2)
        return pltpu.make_async_remote_copy(
            src_ref=source, dst_ref=(sk, sv)[kind].at[slot],
            send_sem=block_s.at[1, head, kind], recv_sem=stop_r.at[slot, kind],
            device_id=dev(target), device_id_type=MESH,
        )

    def relay_up(head):
        for kind in (0, 1):
            held = (rk, rv)[kind].at[0, head]

            @pl.when(z < 3)
            def _():
                block_copy(held, 2, head, kind, around(1)).start()

            @pl.when(z == 3)
            def _():
                stop_copy(held, head, kind, on_line(0)).start()

    def relay_down(head):
        for kind in (0, 1):
            held = (rk, rv)[kind].at[2, head]

            @pl.when(z > 0)
            def _():
                block_copy(held, 2, head, kind, around(-1)).start()

            @pl.when(z == 0)
            def _():
                stop_copy(held, head, kind, on_line(3)).start()

    onward_line = jnp.where(z == 0, around(4), around(-4))
    onward_first = jnp.where(z == 0, 0, 2)

    def onward_copy(slot, kind):
        head = onward_first + slot
        return pltpu.make_async_remote_copy(
            src_ref=(sk, sv)[kind].at[slot], dst_ref=(rk, rv)[kind].at[1, head],
            send_sem=stop_s.at[slot, kind], recv_sem=block_r.at[1, head, kind],
            device_id=dev(onward_line), device_id_type=MESH,
        )

    def hand_on(slot, at):
        @pl.when(z == at)
        def _():
            for kind in (0, 1):
                stop_copy((sk, sv)[kind].at[slot], slot, kind, on_line(0)).wait_recv()
                onward_copy(slot, kind).start()

    for head in chunk_order:
        own_chunk(head, 0).wait()
        own_chunk(head, 1).wait()
        if head == 0:
            own_send(0, 0)
            own_send(0, 1)
    own_send(1, 0)

    running = decay[...]
    shift = 1
    lane = lax.broadcasted_iota(jnp.int32, (KV, T), 1)
    while shift < T:
        running = running + jnp.where(lane >= shift, pltpu.roll(running, shift, 1), 0.0)
        shift *= 2
    id_row = ids[...].astype(F32)
    rows = jnp.concatenate([running, id_row, jnp.zeros((3, T), F32)], 0)
    rows_out[...] = rows
    columns = jnp.concatenate([rows, jnp.zeros((H - 8, T), F32)], 0).T
    id_column = jnp.broadcast_to(columns[:, 4:5], (T, H))
    for head in range(KV):
        cum[head] = jnp.broadcast_to(columns[:, head : head + 1], (T, H))
    for part in range(4):
        row_at = lax.broadcasted_iota(jnp.int32, (T, H), 0)
        column_at = lax.broadcasted_iota(jnp.int32, (T, H), 1) + part * H
        span = slice(part * H, (part + 1) * H)
        linked = (column_at <= row_at) & (id_column == id_row[:, span])
        causal[:, span] = jnp.where(linked, 0.0, HIDDEN)
        later[:, span] = jnp.where(column_at > row_at, 0.0, HIDDEN)
    last_id = id_row[:, T - 1 : T]
    own_tail = id_column == last_id

    relay_four(0, 0)
    for back in (1, 2, 3, 4):
        id_copy(back).wait_recv()
    prev_id = jnp.where(me > 0, rid[0].astype(F32)[:, T - 1 : T], -1.0)
    before = jnp.zeros((1, 1), F32)
    for back in (1, 2, 3, 4):
        same = (rid[back - 1].astype(F32) == prev_id).astype(F32)
        count = jnp.sum(same, axis=1, keepdims=True)
        before = before + jnp.where(me >= back, count, 0.0)
    alive = (id_column == prev_id).astype(F32)
    alive_ref[...] = alive
    lane_at = lax.broadcasted_iota(jnp.int32, (T, H), 1)
    columns_out[...] = jnp.where(
        lane_at == 5, alive, jnp.where(lane_at == 6, jnp.broadcast_to(before, (T, H)), columns)
    )
    own_carry = (last_id == prev_id).astype(F32)

    for head in range(KV):
        end = running[head : head + 1, T - 1 : T]
        weight = jnp.where(own_tail, jnp.exp(end - cum[head]), 0.0)
        weighted = (kb[head].astype(F32) * weight).astype(BF16)
        state = tn(weighted, vb[head])
        factor = jnp.broadcast_to(jnp.exp(end) * own_carry, (1, H))
        sa[head] = pack_state(state, factor)

    def state_copy(stage, source, target, slot, ctx):
        return pltpu.make_async_remote_copy(
            src_ref=source, dst_ref=target.at[slot], send_sem=st_s.at[stage, slot],
            recv_sem=st_r.at[stage, slot], device_id=dev(ctx), device_id_type=MESH,
        )

    def state_send(stage, step):
        if stage == 0:
            to = lax.rem(z + step, 4)
            return pltpu.make_async_remote_copy(
                src_ref=sa.at[to], dst_ref=ra.at[z], send_sem=st_s.at[0, step], recv_sem=st_r.at[0, step],
                device_id=dev(on_line(to)), device_id_type=MESH,
            )
        if stage == 1:
            return pltpu.make_async_remote_copy(
                src_ref=sx, dst_ref=rx.at[x], send_sem=st_s.at[1, step], recv_sem=st_r.at[1, step],
                device_id=dev(on_x(lax.rem(x + step, 4))), device_id_type=MESH,
            )
        if stage == 2:
            return pltpu.make_async_remote_copy(
                src_ref=sy, dst_ref=ry.at[y], send_sem=st_s.at[2, step], recv_sem=st_r.at[2, step],
                device_id=dev(on_y(lax.rem(y + step, 4))), device_id_type=MESH,
            )
        to = lax.rem(z + step, 4)
        return pltpu.make_async_remote_copy(
            src_ref=sd.at[to], dst_ref=rd.at[z], send_sem=st_s.at[3, step], recv_sem=st_r.at[3, step],
            device_id=dev(on_line(to)), device_id_type=MESH,
        )

    def start_stage(stage):
        for step in (1, 2, 3):
            state_send(stage, step).start()

    def finish_stage(stage):
        for step in (1, 2, 3):
            state_send(stage, step).wait_recv()

    ra[z] = sa[z]
    start_stage(0)

    def fold(messages, limit=None):
        state, factor = jnp.zeros((H, H), F32), jnp.ones((1, H), F32)
        for position in range(4):
            item, by = unpack_state(messages[position])
            fresh, grown = state * by + item, factor * by
            if limit is None:
                state, factor = fresh, grown
            else:
                state = jnp.where(position < limit, fresh, state)
        return state, factor

    def after_line():
        finish_stage(0)
        sx[...] = pack_state(*fold(ra))
        rx[x] = sx[...]
        start_stage(1)

    def after_x():
        finish_stage(1)
        sy[...] = pack_state(*fold(rx))
        ry[y] = sy[...]
        start_stage(2)

    def after_y():
        finish_stage(2)
        state, _ = fold(ry, y)
        for position in range(4):
            item, by = unpack_state(rx[position])
            state = jnp.where(position < x, state * by + item, state)
        for position in range(4):
            sd[position] = state.astype(BF16)
            item, by = unpack_state(ra[position])
            state = state * by + item
        rd[z] = sd[z]
        start_stage(3)

    q_copy.wait()

    def own_unit(head):
        keys, values = kb[head], vb[head]
        wide = jnp.concatenate([values, jnp.ones((T, H), BF16)], 1)
        row = rows_out[pl.ds(head, 1), :]
        for first in (0, 256):
            here, upto = slice(first, first + 256), first + 256
            column = cum[head, here, :]
            for part in range(0, upto, H):
                span = slice(part, part + H)
                own_decay[here, span] = jnp.exp(column - row[:, span] + causal[here, span])
        for first in (0, 256):
            here, upto = slice(first, first + 256), first + 256
            for member in range(G):
                at = head_columns(head * G + member)
                scores = nt(q[here, at], keys[:upto])
                grown = jnp.exp2(scores * SCALE + causal[here, :upto]).astype(BF16)
                mixed = nn(grown, wide[:upto])
                acc[here, at] = mixed[:, :H]
                total[here, at] = mixed[:, H:]
                lin[here, at] = nn((scores * own_decay[here, :upto]).astype(BF16), values[:upto])

    def masked_values(back, head):
        place = lax.broadcasted_iota(jnp.int32, (T, H), 0).astype(F32)
        kept = place >= back * float(T) - columns_out[0:1, 6:7]
        values = jnp.where(kept, rv[back - 1, head].astype(F32), 0.0)
        return jnp.concatenate([values, jnp.where(kept, 1.0, 0.0)], 1).astype(BF16)

    def gather(here, at, mixed):
        live = alive_ref[here, :] > 0.0
        acc[here, at] += jnp.where(live, mixed[:, :H], 0.0)
        total[here, at] += jnp.where(live, mixed[:, H:], 0.0)

    def far_unit(back, head):
        keys, wide = rk[back - 1, head], masked_values(back, head)
        for member in range(G):
            at = head_columns(head * G + member)
            grown = jnp.exp2(nt(q[:, at], keys) * SCALE).astype(BF16)
            gather(slice(0, T), at, nn(grown, wide))

    def oldest_unit(head):
        keys, wide = rk[3, head], masked_values(4, head)
        for first in (0, 256):
            here, since = slice(first, first + 256), slice(first, T)
            for member in range(G):
                at = head_columns(head * G + member)
                scores = nt(q[here, at], keys[since])
                grown = jnp.exp2(scores * SCALE + later[here, since]).astype(BF16)
                gather(here, at, nn(grown, wide[since]))

    relay_four(0, 1)
    own_send(1, 1)

    def first_up(head, at_end):
        @pl.when((z == 3) == at_end)
        def _():
            receive(1, head)
            relay_up(head)
            save(1, head)

    def own_step(head, carry):
        own_unit(head)

        @pl.when(head == 0)
        def _():
            own_send(2, 0)

        @pl.when(head == 1)
        def _():
            after_line()
            own_send(2, 1)
            first_up(0, True)

        @pl.when(head == 2)
        def _():
            relay_four(1, 0)
            relay_four(1, 1)
            own_send(3, 0)

        @pl.when(head == 3)
        def _():
            own_send(3, 1)
            first_up(0, False)
            first_up(1, True)

        return carry

    lax.fori_loop(0, KV, own_step, 0)

    def cross():
        finish_stage(3)
        squares[...] = jnp.zeros((T, H), F32)

        def cross_step(head, carry):
            state = rd[head]
            states_in[head] = state.astype(F32)
            entry = jnp.exp(cum[head]) * alive_ref[...]
            part = squares[...]
            for member in range(G):
                at = head_columns(head * G + member)
                whole = lin[:, at] + nn(q[:, at], state) * entry
                lin[:, at] = whole
                part = part + whole * whole
            squares[...] = part
            return carry

        lax.fori_loop(0, KV, cross_step, 0)
        row_sum = jnp.sum(squares[...], axis=1, keepdims=True)
        squares[...] = jnp.broadcast_to(row_sum, (T, H))
        square_copy().start()

    def square_copy():
        return pltpu.make_async_remote_copy(
            src_ref=squares, dst_ref=partner, send_sem=sq_s, recv_sem=sq_r, device_id=other,
            device_id_type=MESH,
        )

    def out_copy(head):
        wide = pl.ds(pl.multiple_of(head * G * H, G * H), G * H)
        return pltpu.make_async_copy(outb.at[:, wide], out_hbm.at[:, wide], out_sem.at[head])

    def listed(step):
        code = jnp.int32(0)
        for place, order in enumerate(ORDERS):
            mine = jnp.int32(0)
            for index, (back, head) in enumerate(order):
                mine = jnp.where(step == index, back * 4 + head, mine)
            code = jnp.where(z == place, mine, code)
        return code // 4, lax.rem(code, 4)

    def far_step(step, carry):
        back, head = listed(step)

        @pl.when(step == 1)
        def _():
            after_x()

        @pl.when(step == 3)
        def _():
            after_y()

        @pl.when(step == 1)
        def _():
            relay_four(2, 0, up=False)
            relay_four(2, 1, up=False)

        @pl.when(step == 2)
        def _():
            relay_four(2, 0, down=False)
            relay_four(2, 1, down=False)
            hand_on(0, 0)

        @pl.when(step == 3)
        def _():
            relay_four(3, 0)
            relay_four(3, 1)

        @pl.when(step == 6)
        def _():
            hand_on(1, 0)
            hand_on(0, 3)

        @pl.when(step == 7)
        def _():
            cross()

        @pl.when(step == 8)
        def _():
            hand_on(1, 3)
            square_copy().wait_recv()
            mean = (squares[...] + partner[...]) * (1.0 / (QUERY_HEADS * HEAD_SIZE))
            inverse_out[...] = lax.rsqrt(mean + 1e-06)
            flag[...] = jnp.zeros((8, H), F32)

        @pl.when((back != 1) | (head > jnp.where(z == 3, 1, 0)))
        def _():
            receive(back, head)
            save(back, head)

        @pl.when((back == 1) & (head == 1) & (z < 3))
        def _():
            relay_up(head)

        @pl.when((back == 3) & (head >= 2))
        def _():
            relay_down(head)

        far_unit(back, head)
        return carry

    def old_step(step, carry):
        oldest_unit(early_head(step))
        lax.fori_loop(2 * step, 2 * step + 2, far_step, 0)
        return carry

    def last_step(step, carry):
        far_step(step, carry)
        head = step - 8
        head = jnp.where((z == 0) & (head > 0) & (head < 3), 3 - head, head)
        for member in range(G):
            at = head_columns(head * G + member)
            mass = total[:, at]
            good = (mass >= SMALL) & (mass <= LARGE)
            flag[...] += jnp.sum(jnp.where(good, 0.0, 1.0).reshape(T // 8, 8, H), axis=0)
            mixed = acc[:, at] / mass + gain[:, at] * (lin[:, at] * inverse_out[...])
            outb[:, at] = mixed.astype(BF16)
        out_copy(head).start()
        return carry

    lax.fori_loop(0, 4, old_step, 0)
    lax.fori_loop(8, 12, last_step, 0)

    for head in range(KV):
        out_copy(head).wait()
        for kind in (0, 1):
            for back in (1, 2, 3, 4):
                held = (rk, rv)[kind].at[back - 1, head]
                pltpu.make_async_copy(
                    held, (k_all, v_all)[kind].at[back - 1, head], save_sem.at[back - 1, head, kind]
                ).wait()
                block_copy(held, back, head, kind, to_four).wait_send()
    for back in (1, 2, 3, 4):
        id_copy(back).wait_send()
    for stage in range(4):
        for step in (1, 2, 3):
            state_send(stage, step).wait_send()
    square_copy().wait_send()

    @pl.when((z == 0) | (z == 3))
    def _():
        for slot in (0, 1):
            for kind in (0, 1):
                onward_copy(slot, kind).wait_send()


def finish_kernel(
    flag, cand, q_hbm, k_hbm, v_hbm, k_all, v_all, states_hbm, inverse_hbm, columns_hbm, rows_hbm, gain_hbm,
    out_hbm, q, ks, vs, outb, states_in, inverse, columns, rows, gain, sems,
):
    bad = jnp.max(flag[...]) > 0.0

    @pl.when(jnp.logical_not(bad))
    def _():
        pieces = [pl.ds(part * (T // 8), T // 8) for part in range(8)]
        arrive = [
            pltpu.make_async_copy(cand.at[piece], outb.at[piece], sems.at[part])
            for part, piece in enumerate(pieces)
        ]
        leave = [
            pltpu.make_async_copy(outb.at[piece], out_hbm.at[piece], sems.at[part])
            for part, piece in enumerate(pieces)
        ]
        for copy in arrive:
            copy.start()
        for there, onward in zip(arrive, leave):
            there.wait()
            onward.start()
        for copy in leave:
            copy.wait()

    @pl.when(bad)
    def _():
        def bring(source, target, sem):
            copy = pltpu.make_async_copy(source, target, sems.at[sem])
            copy.start()
            copy.wait()

        bring(q_hbm, q, 0)
        bring(states_hbm, states_in, 0)
        bring(inverse_hbm, inverse, 0)
        bring(columns_hbm, columns, 0)
        bring(rows_hbm, rows, 0)
        bring(gain_hbm, gain, 0)
        for head in range(KV):
            for source, whole, target in ((k_hbm, k_all, ks), (v_hbm, v_all, vs)):
                bring(source.at[:, pl.ds(head * H, H)], target.at[head, pl.ds(4 * T, T)], 0)
                for back in (1, 2, 3, 4):
                    bring(whole.at[back - 1, head], target.at[head, pl.ds((4 - back) * T, T)], 0)

        def query_step(index, carry):
            head = index // G
            at = head_columns(index)
            for first in range(0, T, 128):
                here = pl.ds(first, 128)
                queries = q[here, at]
                id_column, alive = columns[here, 4:5], columns[here, 5:6]
                before = columns[here, 6:7]
                spot = lax.broadcasted_iota(jnp.int32, (128, 5 * T), 1)
                turn = lax.broadcasted_iota(jnp.int32, (128, 5 * T), 0) + first
                inside = (spot > turn) & (spot <= turn + 4 * T)
                ids = jnp.concatenate([jnp.zeros((1, 4 * T), F32), rows[4:5, :]], 1)
                old = (alive > 0.0) & (spot.astype(F32) >= 4.0 * T - before)
                allowed = inside & (((spot < 4 * T) & old) | ((spot >= 4 * T) & (ids == id_column)))
                scores = nt(queries, ks[head]) * (1.0 / math.sqrt(HEAD_SIZE))
                scores = jnp.where(allowed, scores, HIDDEN)
                top = jnp.max(scores, axis=1, keepdims=True)
                grown = jnp.where(allowed, jnp.exp(scores - top), 0.0)
                weights = grown / jnp.sum(grown, axis=1, keepdims=True)
                window = nn(weights.astype(BF16), vs[head])
                row = rows[pl.ds(head, 1), :]
                lane = lax.broadcasted_iota(jnp.int32, (128, H), 1)
                column = jnp.sum(
                    jnp.where(lane == head, columns[here, :], 0.0), axis=1, keepdims=True
                )
                own_at = lax.broadcasted_iota(jnp.int32, (128, T), 1)
                own_turn = lax.broadcasted_iota(jnp.int32, (128, T), 0) + first
                linked = (own_at <= own_turn) & (rows[4:5, :] == id_column)
                gap = jnp.where(linked, column - row, 0.0)
                kept = jnp.where(linked, jnp.exp(gap), 0.0)
                dots = nt(queries, ks[head, pl.ds(4 * T, T)]) * kept
                linear = nn(dots.astype(BF16), vs[head, pl.ds(4 * T, T)])
                entry = jnp.exp(column) * alive
                linear = linear + nn(queries, states_in[head].astype(BF16)) * entry
                mixed = window + gain[:, at] * (linear * inverse[here, :])
                outb[here, at] = mixed.astype(BF16)
            return carry

        lax.fori_loop(0, KV * G, query_step, 0)
        bring(outb, out_hbm, 0)


def body(queries, keys, values, token_log_decay, seq_ids, norm_gain):
    any_spec = pl.BlockSpec(memory_space=pltpu.HBM)
    vmem_spec = pl.BlockSpec(memory_space=pltpu.VMEM)
    dma = pltpu.SemaphoreType.DMA
    gain = norm_gain.reshape(1, -1)
    ids = seq_ids.reshape(1, -1)
    wide = KV * G * H
    results = pl.pallas_call(
        main_kernel,
        out_shape=(
            jax.ShapeDtypeStruct((T, wide), BF16),
            jax.ShapeDtypeStruct((8, H), F32),
            jax.ShapeDtypeStruct((4, KV, T, H), BF16),
            jax.ShapeDtypeStruct((4, KV, T, H), BF16),
            jax.ShapeDtypeStruct((KV, H, H), F32),
            jax.ShapeDtypeStruct((T, H), F32),
            jax.ShapeDtypeStruct((T, H), F32),
            jax.ShapeDtypeStruct((8, T), F32),
        ),
        in_specs=[any_spec] * 3 + [vmem_spec] * 3,
        out_specs=(any_spec, vmem_spec, any_spec, any_spec, vmem_spec, vmem_spec, vmem_spec, vmem_spec),
        scratch_shapes=[
            pltpu.VMEM((T, wide), BF16),
            pltpu.VMEM((KV, T, H), BF16),
            pltpu.VMEM((KV, T, H), BF16),
            pltpu.VMEM((4, KV, T, H), BF16),
            pltpu.VMEM((4, KV, T, H), BF16),
            pltpu.VMEM((4, 1, T), jnp.int32),
            pltpu.VMEM((T, wide), F32),
            pltpu.VMEM((T, wide), F32),
            pltpu.VMEM((T, wide), F32),
            pltpu.VMEM((T, T), F32),
            pltpu.VMEM((T, T), F32),
            pltpu.VMEM((KV, T, H), F32),
            pltpu.VMEM((T, H), F32),
            pltpu.VMEM((T, H), F32),
            pltpu.VMEM((T, H), F32),
            pltpu.VMEM((4, STATE_ROWS, H), BF16),
            pltpu.VMEM((4, STATE_ROWS, H), BF16),
            pltpu.VMEM((4, STATE_ROWS, H), BF16),
            pltpu.VMEM((4, STATE_ROWS, H), BF16),
            pltpu.VMEM((4, H, H), BF16),
            pltpu.VMEM((4, H, H), BF16),
            pltpu.VMEM((STATE_ROWS, H), BF16),
            pltpu.VMEM((STATE_ROWS, H), BF16),
            pltpu.VMEM((T, wide), BF16),
            pltpu.VMEM((T, T), F32),
            pltpu.VMEM((2, T, H), BF16),
            pltpu.VMEM((2, T, H), BF16),
            dma((KV, 2)),
            dma,
            dma((KV,)),
            dma((4, KV, 2)),
            dma((4,)),
            dma((4,)),
            dma((4, KV, 2)),
            dma((4, KV, 2)),
            dma((4, 4)),
            dma((4, 4)),
            dma,
            dma,
            dma((2, 2)),
            dma((2, 2)),
        ],
        compiler_params=pltpu.CompilerParams(
            collective_id=0, has_side_effects=True, vmem_limit_bytes=56 << 20
        ),
        name="attend",
    )(queries, keys, values, token_log_decay, ids, gain)
    cand, flag, k_all, v_all, states_in, inverse, columns, rows = results
    return pl.pallas_call(
        finish_kernel,
        out_shape=jax.ShapeDtypeStruct((T, wide), BF16),
        in_specs=[vmem_spec] + [any_spec] * 11,
        out_specs=any_spec,
        scratch_shapes=[
            pltpu.VMEM((T, wide), BF16),
            pltpu.VMEM((KV, 5 * T, H), BF16),
            pltpu.VMEM((KV, 5 * T, H), BF16),
            pltpu.VMEM((T, wide), BF16),
            pltpu.VMEM((KV, H, H), F32),
            pltpu.VMEM((T, H), F32),
            pltpu.VMEM((T, H), F32),
            pltpu.VMEM((8, T), F32),
            pltpu.VMEM((1, wide), F32),
            dma((8,)),
        ],
        compiler_params=pltpu.CompilerParams(vmem_limit_bytes=56 << 20),
        name="finish",
    )(flag, cand, queries, keys, values, k_all, v_all, states_in, inverse, columns, rows, gain)


def solution(mesh):
    return jax.shard_map(
        body,
        mesh=mesh,
        in_specs=(
            P("ctx", "head"),
            P("ctx", "head"),
            P("ctx", "head"),
            P("head", "ctx"),
            P("ctx"),
            P("head"),
        ),
        out_specs=P("ctx", "head"),
        check_vma=False,
    )
```
